32 devices in a mesh: tm: 4 (over y, x), tp: 8 (over z, core).
Axes of the slice: x: 2, y: 2, z: 4, core: 2. Of those that a mesh axis runs over, the one named last changes fastest.
Arguments:
- pixels: bfloat16 [8, 32, 32, 1176], P('tm', 'tp'), may hold values from -6 to 6
- conv_weight: bfloat16 [1176, 1280], P(None, 'tm'), may hold values from -0.1875 to 0.1875
- norm_gain: float32 [1280], replicated, may hold values from 0.1 to 1.9
- norm_bias: float32 [1280], replicated, may hold values from -3 to 3
- proj_in: bfloat16 [5120, 5120], P(None, 'tp'), may hold values from -0.078125 to 0.078125
- bias_in: float32 [5120], P('tp'), may hold values from -3 to 3
- proj_out: bfloat16 [5120, 8192], P(None, 'tp'), may hold values from -0.078125 to 0.078125
- bias_out: float32 [8192], P('tp'), may hold values from -3 to 3
Outputs:
- tokens_out: bfloat16 [8, 16, 16, 8192], P('tm', None, None, 'tp')
The draws below stay inside these ranges and needn't reach their ends.
All inputs are finite; a program needn't handle non-finite values.
Results may differ from the reference program's by a relative error of at most 0.0052.
Values may be sent and summed in bfloat16 or wider, within the bound.
A program may use at most 64 MiB of HBM per device.

```python
import jax
import jax.numpy as jnp
from jax import lax

KP = 1176
C = 1280
HID = 5120
OUT = 8192
GH = 32
GW = 32
PAIRS = 8


def block_levels(key, shape, shards, low, top_value):
    loudness = 1.0
    for dim, shards_of in shards:
        draws = jax.random.uniform(jax.random.fold_in(jax.random.fold_in(key, 6), dim), (shards_of,), jnp.float32, low / len(shards), top_value / len(shards))
        loudness = loudness * jnp.repeat(jnp.exp(draws), shape[dim] // shards_of).reshape((-1,) + (1,) * (len(shape) - 1 - dim))
    return loudness


def normal_values(rng, shape, spread, bound, split=(), kind=jnp.bfloat16):
    entries = jax.random.normal(rng, shape, jnp.float32) * spread
    if len(split) > 0:
        entries = block_levels(rng, shape, split, -0.22, 0.18) * entries
    return jnp.clip(entries, min=-bound, max=bound).astype(kind)


def setup_inputs(seed: int = 0) -> dict:
    keys = jax.random.split(jax.random.key(seed), 9)
    pixels = normal_values(keys[0], (PAIRS, GH, GW, KP), 1.0, 6.0, ((0, 4), (1, 8)))
    conv_weight = normal_values(keys[1], (KP, C), KP ** -0.5, 0.1875, ((1, 4),))
    norm_gain = jnp.clip(1.0 + 0.18 * jax.random.normal(keys[2], (C,), jnp.float32), 0.1, 1.9)
    norm_bias = normal_values(keys[3], (C,), 0.3, 3.0, (), jnp.float32)
    proj_in = normal_values(keys[4], (HID, HID), HID ** -0.5, 0.078125, ((1, 8),))
    bias_in = normal_values(keys[5], (HID,), 0.5, 3.0, ((0, 8),), jnp.float32)
    proj_out = normal_values(keys[6], (HID, OUT), HID ** -0.5, 0.078125, ((1, 8),))
    bias_out = normal_values(keys[7], (OUT,), 0.5, 3.0, ((0, 8),), jnp.float32)
    return dict(pixels=pixels, conv_weight=conv_weight, norm_gain=norm_gain, norm_bias=norm_bias, proj_in=proj_in, bias_in=bias_in, proj_out=proj_out, bias_out=bias_out)


def one_pair(frame, conv_weight, norm_gain, norm_bias, proj_in, bias_in, proj_out, bias_out):
    flat = frame.reshape(GH * GW, KP)
    embed = jnp.dot(flat, conv_weight, preferred_element_type=jnp.float32)
    mean = lax.optimization_barrier(jnp.mean(embed, axis=-1, keepdims=True))
    centred = embed - mean
    variance = lax.optimization_barrier(jnp.mean(centred * centred, axis=-1, keepdims=True))
    normed = (centred * lax.rsqrt(variance + 1e-06) * norm_gain + norm_bias).astype(jnp.bfloat16)
    blocks = normed.reshape(GH // 2, 2, GW // 2, 2, C).transpose(0, 2, 1, 3, 4)
    merged = blocks.reshape(GH // 2 * (GW // 2), HID)
    hidden = jax.nn.gelu(jnp.dot(merged, proj_in, preferred_element_type=jnp.float32) + bias_in, approximate=False).astype(jnp.bfloat16)
    result = jnp.dot(hidden, proj_out, preferred_element_type=jnp.float32) + bias_out
    return result.astype(jnp.bfloat16).reshape(GH // 2, GW // 2, OUT)

def reference(pixels, conv_weight, norm_gain, norm_bias, proj_in, bias_in, proj_out, bias_out):

    def step(frame):
        return one_pair(frame, conv_weight, norm_gain, norm_bias, proj_in, bias_in, proj_out, bias_out)
    return lax.map(step, pixels)
```

```python
import jax
import jax.numpy as jnp
from jax import lax
from jax.sharding import PartitionSpec as P


def per_device_split_blocks(pixels, conv_weight, norm_gain, norm_bias, proj_in, bias_in, proj_out, bias_out):
    kernel = lax.all_gather(conv_weight, "tm", axis=1, tiled=True)
    pairs_here, rows_here, cols_all, patch_len = pixels.shape
    channels = kernel.shape[1]
    embed = jnp.dot(pixels.reshape(-1, patch_len), kernel, preferred_element_type=jnp.float32)
    mean = jnp.mean(embed, axis=-1, keepdims=True)
    centred = embed - mean
    variance = jnp.mean(centred * centred, axis=-1, keepdims=True)
    normed = (centred * lax.rsqrt(variance + 1e-06) * norm_gain + norm_bias).astype(jnp.bfloat16)
    normed = normed.reshape(pairs_here, rows_here, cols_all, channels)
    items = normed.reshape(pairs_here, rows_here, cols_all // 2, 2, channels)
    items = items.transpose(0, 2, 1, 3, 4).reshape(
        pairs_here * (cols_all // 2), rows_here, 2, channels
    )
    moved = lax.all_to_all(items, "tp", split_axis=0, concat_axis=1, tiled=True)
    owned = moved.shape[0]
    rows_full = moved.shape[1]
    merged = moved.reshape(owned, rows_full // 2, 2, 2, channels).reshape(
        owned * (rows_full // 2), 4 * channels
    )
    pre = (
        jnp.dot(
            lax.all_gather(merged, "tp", axis=0, tiled=True),
            proj_in,
            preferred_element_type=jnp.float32,
        )
        + bias_in
    )
    hidden = jax.nn.gelu(pre, approximate=False).astype(jnp.bfloat16)
    out_cols = proj_out.shape[1]
    summed = jnp.dot(
        lax.all_gather(hidden, "tp", axis=1, tiled=True),
        proj_out,
        preferred_element_type=jnp.float32,
    )
    result = (summed + bias_out).astype(jnp.bfloat16)
    result = result.reshape(pairs_here, cols_all // 2, rows_full // 2, out_cols).transpose(
        0, 2, 1, 3
    )
    return result


def per_device_whole_blocks(pixels, conv_weight, norm_gain, norm_bias, proj_in, bias_in, proj_out, bias_out):
    kernel = lax.all_gather(conv_weight, "tm", axis=1, tiled=True)
    pairs_here, rows_here, cols_all, patch_len = pixels.shape
    channels = kernel.shape[1]
    embed = jnp.dot(pixels.reshape(-1, patch_len), kernel, preferred_element_type=jnp.float32)
    mean = jnp.mean(embed, axis=-1, keepdims=True)
    centred = embed - mean
    variance = jnp.mean(centred * centred, axis=-1, keepdims=True)
    normed = (centred * lax.rsqrt(variance + 1e-06) * norm_gain + norm_bias).astype(jnp.bfloat16)
    normed = normed.reshape(pairs_here, rows_here, cols_all, channels)
    merged = normed.reshape(pairs_here, rows_here // 2, 2, cols_all // 2, 2, channels)
    merged = merged.transpose(0, 1, 3, 2, 4, 5).reshape(-1, 4 * channels)
    pre = (
        jnp.dot(
            lax.all_gather(merged, "tp", axis=0, tiled=True),
            proj_in,
            preferred_element_type=jnp.float32,
        )
        + bias_in
    )
    hidden = jax.nn.gelu(pre, approximate=False).astype(jnp.bfloat16)
    out_cols = proj_out.shape[1]
    summed = jnp.dot(
        lax.all_gather(hidden, "tp", axis=1, tiled=True),
        proj_out,
        preferred_element_type=jnp.float32,
    )
    result = (summed + bias_out).astype(jnp.bfloat16)
    tp = lax.axis_size("tp")
    result = result.reshape(tp, pairs_here, rows_here // 2, cols_all // 2, out_cols)
    result = result.transpose(1, 0, 2, 3, 4).reshape(
        pairs_here, tp * (rows_here // 2), cols_all // 2, out_cols
    )
    return result


def per_device(pixels, *rest):
    body = per_device_whole_blocks if pixels.shape[1] % 2 == 0 else per_device_split_blocks
    return body(pixels, *rest)


def solution(mesh):
    return jax.shard_map(
        per_device,
        mesh=mesh,
        in_specs=(
            P("tm", "tp", None, None),
            P(None, "tm"),
            P(),
            P(),
            P(None, "tp"),
            P("tp"),
            P(None, "tp"),
            P("tp"),
        ),
        out_specs=P("tm", None, None, "tp"),
        check_vma=False,
    )
```

```python
import functools

import jax
import jax.numpy as jnp
from jax import lax
from jax.experimental import pallas as pl
from jax.experimental.pallas import tpu as pltpu
from jax.sharding import PartitionSpec as P


def per_device_split_blocks(pixels, conv_weight, norm_gain, norm_bias, proj_in, bias_in, proj_out, bias_out):
    kernel = lax.all_gather(conv_weight, "tm", axis=1, tiled=True)
    pairs_here, rows_here, cols_all, patch_len = pixels.shape
    channels = kernel.shape[1]
    embed = jnp.dot(pixels.reshape(-1, patch_len), kernel, preferred_element_type=jnp.float32)
    mean = jnp.mean(embed, axis=-1, keepdims=True)
    centred = embed - mean
    variance = jnp.mean(centred * centred, axis=-1, keepdims=True)
    normed = (centred * lax.rsqrt(variance + 1e-06) * norm_gain + norm_bias).astype(jnp.bfloat16)
    normed = normed.reshape(pairs_here, rows_here, cols_all, channels)
    items = normed.reshape(pairs_here, rows_here, cols_all // 2, 2, channels)
    items = items.transpose(0, 2, 1, 3, 4).reshape(
        pairs_here * (cols_all // 2), rows_here, 2, channels
    )
    moved = lax.all_to_all(items, "tp", split_axis=0, concat_axis=1, tiled=True)
    owned = moved.shape[0]
    rows_full = moved.shape[1]
    merged = moved.reshape(owned, rows_full // 2, 2, 2, channels).reshape(
        owned * (rows_full // 2), 4 * channels
    )
    pre = (
        jnp.dot(
            lax.all_gather(merged, "tp", axis=0, tiled=True),
            proj_in,
            preferred_element_type=jnp.float32,
        )
        + bias_in
    )
    hidden = jax.nn.gelu(pre, approximate=False).astype(jnp.bfloat16)
    out_cols = proj_out.shape[1]
    summed = jnp.dot(
        lax.all_gather(hidden, "tp", axis=1, tiled=True),
        proj_out,
        preferred_element_type=jnp.float32,
    )
    result = (summed + bias_out).astype(jnp.bfloat16)
    result = result.reshape(pairs_here, cols_all // 2, rows_full // 2, out_cols).transpose(
        0, 2, 1, 3
    )
    return result


def per_device_whole_blocks(pixels, conv_weight, norm_gain, norm_bias, proj_in, bias_in, proj_out, bias_out):
    kernel = lax.all_gather(conv_weight, "tm", axis=1, tiled=True)
    pairs_here, rows_here, cols_all, patch_len = pixels.shape
    channels = kernel.shape[1]
    embed = jnp.dot(pixels.reshape(-1, patch_len), kernel, preferred_element_type=jnp.float32)
    mean = jnp.mean(embed, axis=-1, keepdims=True)
    centred = embed - mean
    variance = jnp.mean(centred * centred, axis=-1, keepdims=True)
    normed = (centred * lax.rsqrt(variance + 1e-06) * norm_gain + norm_bias).astype(jnp.bfloat16)
    normed = normed.reshape(pairs_here, rows_here, cols_all, channels)
    merged = normed.reshape(pairs_here, rows_here // 2, 2, cols_all // 2, 2, channels)
    merged = merged.transpose(0, 1, 3, 2, 4, 5).reshape(-1, 4 * channels)
    pre = (
        jnp.dot(
            lax.all_gather(merged, "tp", axis=0, tiled=True),
            proj_in,
            preferred_element_type=jnp.float32,
        )
        + bias_in
    )
    hidden = jax.nn.gelu(pre, approximate=False).astype(jnp.bfloat16)
    out_cols = proj_out.shape[1]
    summed = jnp.dot(
        lax.all_gather(hidden, "tp", axis=1, tiled=True),
        proj_out,
        preferred_element_type=jnp.float32,
    )
    result = (summed + bias_out).astype(jnp.bfloat16)
    tp = lax.axis_size("tp")
    result = result.reshape(tp, pairs_here, rows_here // 2, cols_all // 2, out_cols)
    result = result.transpose(1, 0, 2, 3, 4).reshape(
        pairs_here, tp * (rows_here // 2), cols_all // 2, out_cols
    )
    return result


MESH = pl.DeviceIdType.MESH
EPS = 1e-06
VMEM_BYTES = 60 * 1024 * 1024


def fused_kernel(
    dims,
    x_ref, wide_ref, narrow_ref, gain_ref, shift_ref, bias_in_ref, bias_out_ref, proj_in_ref, proj_out_ref,
    out_ref,
    xs, kernel, narrow, lhs, embed, merged, hidden, win, wout,
    own_sems, win_sems, wout_sem,
    conv_send, conv_recv, conv_fwd_send, conv_fwd_recv,
    x_send, x_recv, m_send, m_recv,
    h_send, h_recv, h_own_send, h_own_recv, h_fwd_send, h_fwd_recv,
):
    tm_n, tp_n, pairs, bands, cols, main, rem, channels = dims
    line_n = tp_n // 2
    blocks = pairs * bands
    line_rows = line_n * cols
    hid_local = proj_in_ref.shape[1]
    wide = wide_ref.shape[1]
    thin = channels // tm_n - wide
    half_wide = wide_ref.shape[0] // 2
    half_narrow = narrow_ref.shape[0] // 2
    tm = lax.axis_index("tm")
    tp = lax.axis_index("tp")
    core = lax.rem(tp, 2)
    z = tp // 2
    sibling = (tm, z * 2 + 1 - core)

    def along_line(d):
        return (tm, lax.rem(z + d, line_n) * 2 + core)

    def along_tm(d):
        return (lax.rem(tm + d, tm_n), tp)

    def remote(src, dst, send, recv, device):
        return pltpu.make_async_remote_copy(
            src_ref=src, dst_ref=dst, send_sem=send, recv_sem=recv, device_id=device, device_id_type=MESH
        )

    barrier = pltpu.get_barrier_semaphore()
    peers = [sibling]
    peers += [along_line(d) for d in range(1, line_n)]
    peers += [along_tm(d) for d in range(1, tm_n)]
    for peer in peers:
        pl.semaphore_signal(barrier, inc=1, device_id=peer, device_id_type=MESH)

    own = [
        pltpu.make_async_copy(wide_ref, kernel.at[:, pl.ds(pl.multiple_of(tm * wide, wide), wide)], own_sems.at[0]),
        pltpu.make_async_copy(narrow_ref, narrow.at[tm], own_sems.at[1]),
    ]
    for s in range(blocks):
        own.append(
            pltpu.make_async_copy(
                x_ref.at[pl.ds(s * cols, cols)],
                xs.at[s, pl.ds(pl.multiple_of(z * cols, cols), cols)],
                own_sems.at[2 + s],
            )
        )
    weights = []
    for q in range(4):
        for t in range(tm_n):
            first = q * channels + t * (wide + thin)
            for src, dst, count in (
                (first, q * channels + t * wide, wide),
                (first + wide, q * channels + tm_n * wide + t * thin, thin),
            ):
                weights.append(
                    pltpu.make_async_copy(
                        proj_in_ref.at[pl.ds(src, count)], win.at[pl.ds(dst, count)], win_sems.at[len(weights)]
                    )
                )
    weights_out = pltpu.make_async_copy(proj_out_ref, wout, wout_sem.at[0])
    for copy in own + weights + [weights_out]:
        copy.start()

    pl.semaphore_wait(barrier, len(peers))

    def wide_part(owner, half):
        return kernel.at[
            pl.ds(pl.multiple_of(half * half_wide, 16), half_wide),
            pl.ds(pl.multiple_of(owner * wide, wide), wide),
        ]

    def narrow_part(owner, half):
        return narrow.at[owner, pl.ds(pl.multiple_of(half * half_narrow, 16), half_narrow)]

    conv = []
    for d in range(1, tm_n):
        i = 2 * (d - 1)
        conv.append(
            remote(
                wide_ref.at[pl.ds(pl.multiple_of(core * half_wide, 16), half_wide)],
                wide_part(tm, core), conv_send.at[i], conv_recv.at[i], along_tm(d),
            )
        )
        conv.append(
            remote(
                narrow_ref.at[pl.ds(pl.multiple_of(core * half_narrow, 16), half_narrow)],
                narrow_part(tm, core), conv_send.at[i + 1], conv_recv.at[i + 1], along_tm(d),
            )
        )
    for copy in conv:
        copy.start()

    def x_part(s, place):
        return xs.at[s, pl.ds(pl.multiple_of(place * cols, cols), cols)]

    pixels = []
    for s in range(blocks):
        for d in range(1, line_n):
            pixels.append(
                remote(
                    x_ref.at[pl.ds(s * cols, cols)], x_part(s, z),
                    x_send.at[s, d - 1], x_recv.at[s, d - 1], along_line(d),
                )
            )
    for copy in pixels:
        copy.start()

    forwards = []
    for d in range(1, tm_n):
        i = 2 * (d - 1)
        owner = lax.rem(tm - d + tm_n, tm_n)
        for k, part in ((i, wide_part(owner, core)), (i + 1, narrow_part(owner, core))):
            remote(part, part, conv_send.at[k], conv_recv.at[k], sibling).wait_recv()
            copy = remote(part, part, conv_fwd_send.at[k], conv_fwd_recv.at[k], sibling)
            copy.start()
            forwards.append(copy)
    for copy in own:
        copy.wait()
    for d in range(1, tm_n):
        i = 2 * (d - 1)
        owner = lax.rem(tm - d + tm_n, tm_n)
        for k, part in ((i, wide_part(owner, 1 - core)), (i + 1, narrow_part(owner, 1 - core))):
            remote(part, part, conv_fwd_send.at[k], conv_fwd_recv.at[k], sibling).wait_recv()

    depth = narrow_ref.shape[0]
    left = lax.broadcasted_iota(jnp.int32, (depth, 2 * thin), 1) < thin
    for t in range(0, tm_n, 2):
        a = narrow[t].astype(jnp.float32)
        b = narrow[t + 1].astype(jnp.float32)
        at = tm_n * wide + t * thin
        kernel[0:depth, at : at + 2 * thin] = jnp.where(left, a, pltpu.roll(b, thin, 1)).astype(jnp.bfloat16)
        kernel[depth:, at : at + 2 * thin] = jnp.where(left, pltpu.roll(a, thin, 1), b).astype(jnp.bfloat16)

    for copy in weights:
        copy.wait()

    lane = lax.broadcasted_iota(jnp.int32, (line_rows, 128), 1)
    mine = pl.ds(pl.multiple_of(core * line_rows, line_rows), line_rows)
    other = pl.ds(pl.multiple_of((1 - core) * line_rows, line_rows), line_rows)
    hid_at = pl.multiple_of(tp * hid_local, 128)

    def h_part(s, owner):
        return hidden.at[s, :, pl.ds(pl.multiple_of(owner * hid_local, 128), hid_local)]

    def first_half(s, carry):
        for d in range(1, line_n):
            part = x_part(s, lax.rem(z - d + line_n, line_n))
            remote(part, part, x_send.at[s, d - 1], x_recv.at[s, d - 1], sibling).wait_recv()
        tail = xs[s, :, 4 * main :].astype(jnp.float32)
        for q in range(4):
            rows = slice(q * line_rows, (q + 1) * line_rows)
            lhs[rows, :main] = xs[s, :, q * main : (q + 1) * main]
            keep = (lane >= q * rem) & (lane < (q + 1) * rem)
            lhs[rows, main:] = jnp.where(keep, tail, 0.0).astype(jnp.bfloat16)
        for n in range(0, channels, 256):
            embed[:, n : n + 256] = jnp.dot(lhs[...], kernel[:, n : n + 256], preferred_element_type=jnp.float32)
        for q in range(4):
            value = embed[q * line_rows : (q + 1) * line_rows, :]
            mean = jnp.sum(value, axis=1, keepdims=True) * (1.0 / channels)
            centred = value - mean
            variance = jnp.sum(centred * centred, axis=1, keepdims=True) * (1.0 / channels)
            normed = centred * lax.rsqrt(variance + EPS) * gain_ref[...] + shift_ref[...]
            merged[s, mine, q * channels : (q + 1) * channels] = normed.astype(jnp.bfloat16)
        to_sibling = remote(merged.at[s, mine], merged.at[s, mine], m_send.at[s], m_recv.at[s], sibling)
        to_sibling.start()
        remote(merged.at[s, other], merged.at[s, other], m_send.at[s], m_recv.at[s], sibling).wait_recv()
        pre = jnp.dot(merged[s], win[...], preferred_element_type=jnp.float32) + bias_in_ref[...]
        act = 0.5 * pre * (1.0 + lax.erf(pre * (0.5**0.5)))
        hidden[s, :, pl.ds(hid_at, hid_local)] = act.astype(jnp.bfloat16)
        for d in range(1, line_n):
            remote(h_part(s, tp), h_part(s, tp), h_send.at[s, d - 1], h_recv.at[s, d - 1], along_line(d)).start()
        remote(h_part(s, tp), h_part(s, tp), h_own_send.at[s], h_own_recv.at[s], sibling).start()
        return carry

    lax.fori_loop(0, blocks, first_half, 0)
    weights_out.wait()

    def line_owner(d, which):
        return lax.rem(z - d + line_n, line_n) * 2 + which

    def hand_over(s):
        for d in range(1, line_n):
            part = h_part(s, line_owner(d, core))
            remote(part, part, h_send.at[s, d - 1], h_recv.at[s, d - 1], sibling).wait_recv()
            remote(part, part, h_fwd_send.at[s, d - 1], h_fwd_recv.at[s, d - 1], sibling).start()

    def second_half(s):
        part = h_part(s, z * 2 + 1 - core)
        remote(part, part, h_own_send.at[s], h_own_recv.at[s], sibling).wait_recv()
        for d in range(1, line_n):
            part = h_part(s, line_owner(d, 1 - core))
            remote(part, part, h_fwd_send.at[s, d - 1], h_fwd_recv.at[s, d - 1], sibling).wait_recv()
        pair, band = s // bands, lax.rem(s, bands)
        for n in range(0, out_ref.shape[1], 256):
            total = jnp.dot(hidden[s], wout[:, n : n + 256], preferred_element_type=jnp.float32)
            result = (total + bias_out_ref[:, n : n + 256]).astype(jnp.bfloat16)
            for c in range(2):
                for l in range(line_n):
                    at = ((pair * tp_n + l * 2 + c) * bands + band) * cols
                    r = (c * line_n + l) * cols
                    out_ref[pl.ds(pl.multiple_of(at, cols), cols), n : n + 256] = result[r : r + cols]

    hand_over(0)

    def finish(s, carry):
        hand_over(s)
        second_half(s - 1)
        return carry

    lax.fori_loop(1, blocks, finish, 0)
    second_half(blocks - 1)

    for copy in conv + forwards + pixels:
        copy.wait_send()

    def drain(s, carry):
        remote(merged.at[s, mine], merged.at[s, mine], m_send.at[s], m_recv.at[s], sibling).wait_send()
        remote(h_part(s, tp), h_part(s, tp), h_own_send.at[s], h_own_recv.at[s], sibling).wait_send()
        for d in range(1, line_n):
            part = h_part(s, tp)
            remote(part, part, h_send.at[s, d - 1], h_recv.at[s, d - 1], along_line(d)).wait_send()
            part = h_part(s, line_owner(d, core))
            remote(part, part, h_fwd_send.at[s, d - 1], h_fwd_recv.at[s, d - 1], sibling).wait_send()
        return carry

    lax.fori_loop(0, blocks, drain, 0)


def split_channels(vector, shards, wide):
    parts = vector.reshape(shards, -1)
    return jnp.concatenate([parts[:, :wide].reshape(-1), parts[:, wide:].reshape(-1)]).reshape(1, -1)


def per_device_fused(pixels, conv_weight, norm_gain, norm_bias, proj_in, bias_in, proj_out, bias_out):
    tm_n, tp_n = lax.axis_size("tm"), lax.axis_size("tp")
    pairs, rows, grid_cols, patch = pixels.shape
    channels = conv_weight.shape[1] * tm_n
    bands, cols = rows // 2, grid_cols // 2
    main = patch // 128 * 128
    rem = patch - main
    wide = conv_weight.shape[1] // 256 * 256
    depth = main + 128

    x = pixels.reshape(pairs, bands, 2, cols, 2, patch).transpose(0, 1, 3, 2, 4, 5).reshape(-1, 4, patch)
    n_rows = x.shape[0]
    x = jnp.concatenate(
        [
            x[:, :, :main].reshape(n_rows, 4 * main),
            x[:, :, main:].reshape(n_rows, 4 * rem),
            jnp.zeros((n_rows, 128 - 4 * rem), x.dtype),
        ],
        axis=1,
    )
    w_rem = conv_weight[main:]
    w = jnp.concatenate(
        [conv_weight[:main]] + [w_rem] * 4 + [jnp.zeros((128 - 4 * rem, w_rem.shape[1]), w_rem.dtype)], axis=0
    )
    w_wide = w[:, :wide]
    w_narrow = jnp.concatenate([w[: depth // 2, wide:], w[depth // 2 :, wide:]], axis=1)

    blocks = pairs * bands
    line_n = tp_n // 2
    group = tp_n * cols
    bf16 = jnp.bfloat16
    dma = pltpu.SemaphoreType.DMA
    vmem = pl.BlockSpec(memory_space=pltpu.VMEM)
    anywhere = pl.BlockSpec(memory_space=pl.ANY)
    conv_sems = [dma((2 * (tm_n - 1),))] * 4
    line_sems = dma((blocks, line_n - 1))
    out = pl.pallas_call(
        functools.partial(fused_kernel, (tm_n, tp_n, pairs, bands, cols, main, rem, channels)),
        out_shape=jax.ShapeDtypeStruct((blocks * group, proj_out.shape[1]), bf16),
        in_specs=[vmem] * 7 + [anywhere] * 2,
        out_specs=vmem,
        scratch_shapes=[
            pltpu.VMEM((blocks, line_n * cols, x.shape[1]), bf16),
            pltpu.VMEM((depth, channels), bf16),
            pltpu.VMEM((tm_n,) + w_narrow.shape, bf16),
            pltpu.VMEM((4 * line_n * cols, depth), bf16),
            pltpu.VMEM((4 * line_n * cols, channels), jnp.float32),
            pltpu.VMEM((blocks, group, 4 * channels), bf16),
            pltpu.VMEM((blocks, group, proj_out.shape[0]), bf16),
            pltpu.VMEM(proj_in.shape, bf16),
            pltpu.VMEM(proj_out.shape, bf16),
            dma((2 + blocks,)),
            dma((8 * tm_n,)),
            dma((1,)),
        ]
        + conv_sems
        + [line_sems] * 2
        + [dma((blocks,))] * 2
        + [line_sems] * 2
        + [dma((blocks,))] * 2
        + [line_sems] * 2,
        compiler_params=pltpu.CompilerParams(
            collective_id=0, has_side_effects=True, vmem_limit_bytes=VMEM_BYTES
        ),
    )(
        x, w_wide, w_narrow,
        split_channels(norm_gain, tm_n, wide), split_channels(norm_bias, tm_n, wide),
        bias_in.reshape(1, -1), bias_out.reshape(1, -1), proj_in, proj_out,
    )
    return out.reshape(pairs, tp_n * bands, cols, proj_out.shape[1])


def fused_fits(pixels, conv_weight, proj_in, proj_out):
    pairs, rows, grid_cols, patch = pixels.shape
    tm_n, tp_n = lax.axis_size("tm"), lax.axis_size("tp")
    local = conv_weight.shape[1]
    held = 2 * (proj_in.size + proj_out.size) + 8 * pairs * tp_n * rows * grid_cols * local * tm_n // 2
    return (
        rows % 2 == 0
        and grid_cols % 32 == 0
        and tm_n % 2 == 0
        and tp_n % 2 == 0
        and tp_n >= 4
        and local % 256 == 64
        and patch % 128 != 0
        and 4 * (patch % 128) <= 128
        and proj_in.shape[1] % 128 == 0
        and proj_out.shape[1] % 256 == 0
        and held < VMEM_BYTES // 3 * 2
    )


def per_device(pixels, conv_weight, norm_gain, norm_bias, proj_in, bias_in, proj_out, bias_out):
    if fused_fits(pixels, conv_weight, proj_in, proj_out):
        body = per_device_fused
    elif pixels.shape[1] % 2 == 0:
        body = per_device_whole_blocks
    else:
        body = per_device_split_blocks
    return body(pixels, conv_weight, norm_gain, norm_bias, proj_in, bias_in, proj_out, bias_out)


def solution(mesh):
    return jax.shard_map(
        per_device,
        mesh=mesh,
        in_specs=(
            P("tm", "tp", None, None),
            P(None, "tm"),
            P(),
            P(),
            P(None, "tp"),
            P("tp"),
            P(None, "tp"),
            P("tp"),
        ),
        out_specs=P("tm", None, None, "tp"),
        check_vma=False,
    )
```

```python
import functools

import jax
import jax.numpy as jnp
from jax import lax
from jax.experimental import pallas as pl
from jax.experimental.pallas import tpu as pltpu
from jax.sharding import PartitionSpec as P


def per_device_split_blocks(pixels, conv_weight, norm_gain, norm_bias, proj_in, bias_in, proj_out, bias_out):
    kernel = lax.all_gather(conv_weight, "tm", axis=1, tiled=True)
    pairs_here, rows_here, cols_all, patch_len = pixels.shape
    channels = kernel.shape[1]
    embed = jnp.dot(pixels.reshape(-1, patch_len), kernel, preferred_element_type=jnp.float32)
    mean = jnp.mean(embed, axis=-1, keepdims=True)
    centred = embed - mean
    variance = jnp.mean(centred * centred, axis=-1, keepdims=True)
    normed = (centred * lax.rsqrt(variance + 1e-06) * norm_gain + norm_bias).astype(jnp.bfloat16)
    normed = normed.reshape(pairs_here, rows_here, cols_all, channels)
    items = normed.reshape(pairs_here, rows_here, cols_all // 2, 2, channels)
    items = items.transpose(0, 2, 1, 3, 4).reshape(
        pairs_here * (cols_all // 2), rows_here, 2, channels
    )
    moved = lax.all_to_all(items, "tp", split_axis=0, concat_axis=1, tiled=True)
    owned = moved.shape[0]
    rows_full = moved.shape[1]
    merged = moved.reshape(owned, rows_full // 2, 2, 2, channels).reshape(
        owned * (rows_full // 2), 4 * channels
    )
    pre = (
        jnp.dot(
            lax.all_gather(merged, "tp", axis=0, tiled=True),
            proj_in,
            preferred_element_type=jnp.float32,
        )
        + bias_in
    )
    hidden = jax.nn.gelu(pre, approximate=False).astype(jnp.bfloat16)
    out_cols = proj_out.shape[1]
    summed = jnp.dot(
        lax.all_gather(hidden, "tp", axis=1, tiled=True),
        proj_out,
        preferred_element_type=jnp.float32,
    )
    result = (summed + bias_out).astype(jnp.bfloat16)
    result = result.reshape(pairs_here, cols_all // 2, rows_full // 2, out_cols).transpose(
        0, 2, 1, 3
    )
    return result


def per_device_whole_blocks(pixels, conv_weight, norm_gain, norm_bias, proj_in, bias_in, proj_out, bias_out):
    kernel = lax.all_gather(conv_weight, "tm", axis=1, tiled=True)
    pairs_here, rows_here, cols_all, patch_len = pixels.shape
    channels = kernel.shape[1]
    embed = jnp.dot(pixels.reshape(-1, patch_len), kernel, preferred_element_type=jnp.float32)
    mean = jnp.mean(embed, axis=-1, keepdims=True)
    centred = embed - mean
    variance = jnp.mean(centred * centred, axis=-1, keepdims=True)
    normed = (centred * lax.rsqrt(variance + 1e-06) * norm_gain + norm_bias).astype(jnp.bfloat16)
    normed = normed.reshape(pairs_here, rows_here, cols_all, channels)
    merged = normed.reshape(pairs_here, rows_here // 2, 2, cols_all // 2, 2, channels)
    merged = merged.transpose(0, 1, 3, 2, 4, 5).reshape(-1, 4 * channels)
    pre = (
        jnp.dot(
            lax.all_gather(merged, "tp", axis=0, tiled=True),
            proj_in,
            preferred_element_type=jnp.float32,
        )
        + bias_in
    )
    hidden = jax.nn.gelu(pre, approximate=False).astype(jnp.bfloat16)
    out_cols = proj_out.shape[1]
    summed = jnp.dot(
        lax.all_gather(hidden, "tp", axis=1, tiled=True),
        proj_out,
        preferred_element_type=jnp.float32,
    )
    result = (summed + bias_out).astype(jnp.bfloat16)
    tp = lax.axis_size("tp")
    result = result.reshape(tp, pairs_here, rows_here // 2, cols_all // 2, out_cols)
    result = result.transpose(1, 0, 2, 3, 4).reshape(
        pairs_here, tp * (rows_here // 2), cols_all // 2, out_cols
    )
    return result


MESH = pl.DeviceIdType.MESH
EPS = 1e-06
VMEM_BYTES = 60 * 1024 * 1024


def fused_kernel(
    dims,
    x_ref, wide_ref, narrow_ref, gain_ref, shift_ref, bias_in_ref, bias_out_ref, proj_in_ref, proj_out_ref,
    out_ref,
    xs, kernel, narrow, lhs, embed, merged, hidden, win, wout,
    own_sems, win_sems, wout_sem,
    conv_send, conv_recv, conv_fwd_send, conv_fwd_recv,
    x_send, x_recv, m_send, m_recv,
    h_send, h_recv, h_own_send, h_own_recv, h_fwd_send, h_fwd_recv,
):
    tm_n, tp_n, pairs, bands, cols, main, rem, channels = dims
    line_n = tp_n // 2
    blocks = pairs * bands
    line_rows = line_n * cols
    hid_local = proj_in_ref.shape[1]
    wide = wide_ref.shape[1]
    thin = channels // tm_n - wide
    half_wide = wide_ref.shape[0] // 2
    half_narrow = narrow_ref.shape[0] // 2
    tm = lax.axis_index("tm")
    tp = lax.axis_index("tp")
    core = lax.rem(tp, 2)
    z = tp // 2
    sibling = (tm, z * 2 + 1 - core)

    def on_line(place):
        return (tm, place * 2 + core)

    last = line_n - 1
    inner = (z > 0) & (z < last)
    far_source = (2 - z) * last
    far_target = (z - 1) * last

    def each_reach(act):
        for e in (2, -2, 1, -1):
            place = z + e
            pl.when((place >= 0) & (place <= last))(functools.partial(act, place))

    def each_source(act):
        for place in range(line_n):
            pl.when(z != place)(functools.partial(act, place))

    def along_tm(d):
        return (lax.rem(tm + d, tm_n), tp)

    def remote(src, dst, send, recv, device):
        return pltpu.make_async_remote_copy(
            src_ref=src, dst_ref=dst, send_sem=send, recv_sem=recv, device_id=device, device_id_type=MESH
        )

    barrier = pltpu.get_barrier_semaphore()
    peers = [sibling]
    peers += [on_line(lax.rem(z + d, line_n)) for d in range(1, line_n)]
    peers += [along_tm(d) for d in range(1, tm_n)]
    for peer in peers:
        pl.semaphore_signal(barrier, inc=1, device_id=peer, device_id_type=MESH)

    own = [
        pltpu.make_async_copy(wide_ref, kernel.at[:, pl.ds(pl.multiple_of(tm * wide, wide), wide)], own_sems.at[0]),
        pltpu.make_async_copy(narrow_ref, narrow.at[tm], own_sems.at[1]),
    ]
    for s in range(blocks):
        own.append(
            pltpu.make_async_copy(
                x_ref.at[pl.ds(s * cols, cols)],
                xs.at[s, pl.ds(pl.multiple_of(z * cols, cols), cols)],
                own_sems.at[2 + s],
            )
        )
    weights = []
    for q in range(4):
        for t in range(tm_n):
            first = q * channels + t * (wide + thin)
            for src, dst, count in (
                (first, q * channels + t * wide, wide),
                (first + wide, q * channels + tm_n * wide + t * thin, thin),
            ):
                weights.append(
                    pltpu.make_async_copy(
                        proj_in_ref.at[pl.ds(src, count)], win.at[pl.ds(dst, count)], win_sems.at[len(weights)]
                    )
                )
    weights_out = pltpu.make_async_copy(proj_out_ref, wout, wout_sem.at[0])
    for copy in own + weights + [weights_out]:
        copy.start()

    pl.semaphore_wait(barrier, len(peers))

    def wide_part(owner, half):
        return kernel.at[
            pl.ds(pl.multiple_of(half * half_wide, 16), half_wide),
            pl.ds(pl.multiple_of(owner * wide, wide), wide),
        ]

    def narrow_part(owner, half):
        return narrow.at[owner, pl.ds(pl.multiple_of(half * half_narrow, 16), half_narrow)]

    conv = []
    for d in range(1, tm_n):
        i = 2 * (d - 1)
        conv.append(
            remote(
                wide_ref.at[pl.ds(pl.multiple_of(core * half_wide, 16), half_wide)],
                wide_part(tm, core), conv_send.at[i], conv_recv.at[i], along_tm(d),
            )
        )
        conv.append(
            remote(
                narrow_ref.at[pl.ds(pl.multiple_of(core * half_narrow, 16), half_narrow)],
                narrow_part(tm, core), conv_send.at[i + 1], conv_recv.at[i + 1], along_tm(d),
            )
        )
    def x_part(s, place):
        return xs.at[s, pl.ds(pl.multiple_of(place * cols, cols), cols)]

    def x_copy(s, place):
        return remote(
            x_ref.at[pl.ds(s * cols, cols)], x_part(s, z), x_send.at[s, place], x_recv.at[s, z], on_line(place)
        )

    def x_arrival(s, place):
        return remote(x_part(s, place), x_part(s, place), x_send.at[s, place], x_recv.at[s, place], sibling)

    def x_pass_on(s):
        part = x_part(s, far_source)
        return remote(part, part, x_send.at[s, z], x_recv.at[s, far_source], on_line(far_target))

    def pass_on_pixels(s):
        @pl.when(inner)
        def _():
            x_arrival(s, far_source).wait_recv()
            x_pass_on(s).start()

    for s in range(blocks):
        each_reach(lambda place, s=s: x_copy(s, place).start())
        for copy in conv[2 * s : 2 * s + 2]:
            copy.start()
    for copy in conv[2 * blocks :]:
        copy.start()
    pass_on_pixels(0)

    forwards = []
    for d in range(1, tm_n):
        i = 2 * (d - 1)
        owner = lax.rem(tm - d + tm_n, tm_n)
        for k, part in ((i, wide_part(owner, core)), (i + 1, narrow_part(owner, core))):
            remote(part, part, conv_send.at[k], conv_recv.at[k], sibling).wait_recv()
            copy = remote(part, part, conv_fwd_send.at[k], conv_fwd_recv.at[k], sibling)
            copy.start()
            forwards.append(copy)
    for copy in own:
        copy.wait()
    for d in range(1, tm_n):
        i = 2 * (d - 1)
        owner = lax.rem(tm - d + tm_n, tm_n)
        for k, part in ((i, wide_part(owner, 1 - core)), (i + 1, narrow_part(owner, 1 - core))):
            remote(part, part, conv_fwd_send.at[k], conv_fwd_recv.at[k], sibling).wait_recv()

    depth = narrow_ref.shape[0]
    left = lax.broadcasted_iota(jnp.int32, (depth, 2 * thin), 1) < thin
    for t in range(0, tm_n, 2):
        a = narrow[t].astype(jnp.float32)
        b = narrow[t + 1].astype(jnp.float32)
        at = tm_n * wide + t * thin
        kernel[0:depth, at : at + 2 * thin] = jnp.where(left, a, pltpu.roll(b, thin, 1)).astype(jnp.bfloat16)
        kernel[depth:, at : at + 2 * thin] = jnp.where(left, pltpu.roll(a, thin, 1), b).astype(jnp.bfloat16)

    for copy in weights:
        copy.wait()
    pass_on_pixels(1)

    lane = lax.broadcasted_iota(jnp.int32, (line_rows, 128), 1)
    mine = pl.ds(pl.multiple_of(core * line_rows, line_rows), line_rows)
    other = pl.ds(pl.multiple_of((1 - core) * line_rows, line_rows), line_rows)
    hid_at = pl.multiple_of(tp * hid_local, 128)

    def h_part(s, owner):
        return hidden.at[s, :, pl.ds(pl.multiple_of(owner * hid_local, 128), hid_local)]

    def h_copy(s, place):
        return remote(h_part(s, tp), h_part(s, tp), h_send.at[s, place], h_recv.at[s, z], on_line(place))

    def h_arrival(s, place):
        part = h_part(s, place * 2 + core)
        return remote(part, part, h_send.at[s, place], h_recv.at[s, place], sibling)

    def h_pass_on(s):
        part = h_part(s, far_source * 2 + core)
        return remote(part, part, h_send.at[s, z], h_recv.at[s, far_source], on_line(far_target))

    def h_across(s, place, which):
        part = h_part(s, place * 2 + which)
        return remote(part, part, h_fwd_send.at[s, place], h_fwd_recv.at[s, place], sibling)

    def first_half(s, carry):
        def arrived(place):
            pl.when(jnp.logical_not(inner & (far_source == place)))(lambda: x_arrival(s, place).wait_recv())

        each_source(arrived)
        tail = xs[s, :, 4 * main :].astype(jnp.float32)
        for q in range(4):
            rows = slice(q * line_rows, (q + 1) * line_rows)
            lhs[rows, :main] = xs[s, :, q * main : (q + 1) * main]
            keep = (lane >= q * rem) & (lane < (q + 1) * rem)
            lhs[rows, main:] = jnp.where(keep, tail, 0.0).astype(jnp.bfloat16)
        for n in range(0, channels, 256):
            embed[:, n : n + 256] = jnp.dot(lhs[...], kernel[:, n : n + 256], preferred_element_type=jnp.float32)
        for q in range(4):
            value = embed[q * line_rows : (q + 1) * line_rows, :]
            mean = jnp.sum(value, axis=1, keepdims=True) * (1.0 / channels)
            centred = value - mean
            variance = jnp.sum(centred * centred, axis=1, keepdims=True) * (1.0 / channels)
            normed = centred * lax.rsqrt(variance + EPS) * gain_ref[...] + shift_ref[...]
            merged[s, mine, q * channels : (q + 1) * channels] = normed.astype(jnp.bfloat16)
        to_sibling = remote(merged.at[s, mine], merged.at[s, mine], m_send.at[s], m_recv.at[s], sibling)
        to_sibling.start()
        remote(merged.at[s, other], merged.at[s, other], m_send.at[s], m_recv.at[s], sibling).wait_recv()
        pre = jnp.dot(merged[s], win[...], preferred_element_type=jnp.float32) + bias_in_ref[...]
        act = 0.5 * pre * (1.0 + lax.erf(pre * (0.5**0.5)))
        hidden[s, :, pl.ds(hid_at, hid_local)] = act.astype(jnp.bfloat16)
        each_reach(lambda place: h_copy(s, place).start())
        remote(h_part(s, tp), h_part(s, tp), h_own_send.at[s], h_own_recv.at[s], sibling).start()
        pl.when(s + 2 < blocks)(lambda: pass_on_pixels(s + 2))
        return carry

    lax.fori_loop(0, blocks, first_half, 0)
    weights_out.wait()

    def hand_over(s):
        @pl.when(inner)
        def _():
            h_arrival(s, far_source).wait_recv()
            h_pass_on(s).start()
            h_across(s, far_source, core).start()

        def arrived(place):
            @pl.when(jnp.logical_not(inner & (far_source == place)))
            def _():
                h_arrival(s, place).wait_recv()
                h_across(s, place, core).start()

        each_source(arrived)

    def second_half(s):
        part = h_part(s, z * 2 + 1 - core)
        remote(part, part, h_own_send.at[s], h_own_recv.at[s], sibling).wait_recv()
        each_source(lambda place: h_across(s, place, 1 - core).wait_recv())
        pair, band = s // bands, lax.rem(s, bands)
        for n in range(0, out_ref.shape[1], 256):
            total = jnp.dot(hidden[s], wout[:, n : n + 256], preferred_element_type=jnp.float32)
            result = (total + bias_out_ref[:, n : n + 256]).astype(jnp.bfloat16)
            for c in range(2):
                for l in range(line_n):
                    at = ((pair * tp_n + l * 2 + c) * bands + band) * cols
                    r = (c * line_n + l) * cols
                    out_ref[pl.ds(pl.multiple_of(at, cols), cols), n : n + 256] = result[r : r + cols]

    hand_over(0)

    def finish(s, carry):
        hand_over(s)
        second_half(s - 1)
        return carry

    lax.fori_loop(1, blocks, finish, 0)
    second_half(blocks - 1)

    for copy in conv + forwards:
        copy.wait_send()

    def drain(s, carry):
        remote(merged.at[s, mine], merged.at[s, mine], m_send.at[s], m_recv.at[s], sibling).wait_send()
        remote(h_part(s, tp), h_part(s, tp), h_own_send.at[s], h_own_recv.at[s], sibling).wait_send()
        each_reach(lambda place: x_copy(s, place).wait_send())
        each_reach(lambda place: h_copy(s, place).wait_send())
        each_source(lambda place: h_across(s, place, core).wait_send())

        @pl.when(inner)
        def _():
            x_pass_on(s).wait_send()
            h_pass_on(s).wait_send()

        return carry

    lax.fori_loop(0, blocks, drain, 0)


def split_channels(vector, shards, wide):
    parts = vector.reshape(shards, -1)
    return jnp.concatenate([parts[:, :wide].reshape(-1), parts[:, wide:].reshape(-1)]).reshape(1, -1)


def per_device_fused(pixels, conv_weight, norm_gain, norm_bias, proj_in, bias_in, proj_out, bias_out):
    tm_n, tp_n = lax.axis_size("tm"), lax.axis_size("tp")
    pairs, rows, grid_cols, patch = pixels.shape
    channels = conv_weight.shape[1] * tm_n
    bands, cols = rows // 2, grid_cols // 2
    main = patch // 128 * 128
    rem = patch - main
    wide = conv_weight.shape[1] // 256 * 256
    depth = main + 128

    x = pixels.reshape(pairs, bands, 2, cols, 2, patch).transpose(0, 1, 3, 2, 4, 5).reshape(-1, 4, patch)
    n_rows = x.shape[0]
    x = jnp.concatenate(
        [
            x[:, :, :main].reshape(n_rows, 4 * main),
            x[:, :, main:].reshape(n_rows, 4 * rem),
            jnp.zeros((n_rows, 128 - 4 * rem), x.dtype),
        ],
        axis=1,
    )
    w_rem = conv_weight[main:]
    w = jnp.concatenate(
        [conv_weight[:main]] + [w_rem] * 4 + [jnp.zeros((128 - 4 * rem, w_rem.shape[1]), w_rem.dtype)], axis=0
    )
    w_wide = w[:, :wide]
    w_narrow = jnp.concatenate([w[: depth // 2, wide:], w[depth // 2 :, wide:]], axis=1)

    blocks = pairs * bands
    line_n = tp_n // 2
    group = tp_n * cols
    bf16 = jnp.bfloat16
    dma = pltpu.SemaphoreType.DMA
    vmem = pl.BlockSpec(memory_space=pltpu.VMEM)
    anywhere = pl.BlockSpec(memory_space=pl.ANY)
    conv_sems = [dma((2 * (tm_n - 1),))] * 4
    line_sems = dma((blocks, line_n))
    out = pl.pallas_call(
        functools.partial(fused_kernel, (tm_n, tp_n, pairs, bands, cols, main, rem, channels)),
        out_shape=jax.ShapeDtypeStruct((blocks * group, proj_out.shape[1]), bf16),
        in_specs=[vmem] * 7 + [anywhere] * 2,
        out_specs=vmem,
        scratch_shapes=[
            pltpu.VMEM((blocks, line_n * cols, x.shape[1]), bf16),
            pltpu.VMEM((depth, channels), bf16),
            pltpu.VMEM((tm_n,) + w_narrow.shape, bf16),
            pltpu.VMEM((4 * line_n * cols, depth), bf16),
            pltpu.VMEM((4 * line_n * cols, channels), jnp.float32),
            pltpu.VMEM((blocks, group, 4 * channels), bf16),
            pltpu.VMEM((blocks, group, proj_out.shape[0]), bf16),
            pltpu.VMEM(proj_in.shape, bf16),
            pltpu.VMEM(proj_out.shape, bf16),
            dma((2 + blocks,)),
            dma((8 * tm_n,)),
            dma((1,)),
        ]
        + conv_sems
        + [line_sems] * 2
        + [dma((blocks,))] * 2
        + [line_sems] * 2
        + [dma((blocks,))] * 2
        + [line_sems] * 2,
        compiler_params=pltpu.CompilerParams(
            collective_id=0, has_side_effects=True, vmem_limit_bytes=VMEM_BYTES
        ),
    )(
        x, w_wide, w_narrow,
        split_channels(norm_gain, tm_n, wide), split_channels(norm_bias, tm_n, wide),
        bias_in.reshape(1, -1), bias_out.reshape(1, -1), proj_in, proj_out,
    )
    return out.reshape(pairs, tp_n * bands, cols, proj_out.shape[1])


def fused_fits(pixels, conv_weight, proj_in, proj_out):
    pairs, rows, grid_cols, patch = pixels.shape
    tm_n, tp_n = lax.axis_size("tm"), lax.axis_size("tp")
    local = conv_weight.shape[1]
    held = 2 * (proj_in.size + proj_out.size) + 8 * pairs * tp_n * rows * grid_cols * local * tm_n // 2
    return (
        rows % 2 == 0
        and grid_cols % 32 == 0
        and tm_n % 2 == 0
        and tp_n % 2 == 0
        and tp_n == 8
        and pairs * rows >= 4
        and local % 256 == 64
        and patch % 128 != 0
        and 4 * (patch % 128) <= 128
        and proj_in.shape[1] % 128 == 0
        and proj_out.shape[1] % 256 == 0
        and held < VMEM_BYTES // 3 * 2
    )


def per_device(pixels, conv_weight, norm_gain, norm_bias, proj_in, bias_in, proj_out, bias_out):
    if fused_fits(pixels, conv_weight, proj_in, proj_out):
        body = per_device_fused
    elif pixels.shape[1] % 2 == 0:
        body = per_device_whole_blocks
    else:
        body = per_device_split_blocks
    return body(pixels, conv_weight, norm_gain, norm_bias, proj_in, bias_in, proj_out, bias_out)


def solution(mesh):
    return jax.shard_map(
        per_device,
        mesh=mesh,
        in_specs=(
            P("tm", "tp", None, None),
            P(None, "tm"),
            P(),
            P(),
            P(None, "tp"),
            P("tp"),
            P(None, "tp"),
            P("tp"),
        ),
        out_specs=P("tm", None, None, "tp"),
        check_vma=False,
    )
```

```python
import functools

import jax
import jax.numpy as jnp
from jax import lax
from jax.experimental import pallas as pl
from jax.experimental.pallas import tpu as pltpu
from jax.sharding import PartitionSpec as P


def per_device_split_blocks(pixels, conv_weight, norm_gain, norm_bias, proj_in, bias_in, proj_out, bias_out):
    kernel = lax.all_gather(conv_weight, "tm", axis=1, tiled=True)
    pairs_here, rows_here, cols_all, patch_len = pixels.shape
    channels = kernel.shape[1]
    embed = jnp.dot(pixels.reshape(-1, patch_len), kernel, preferred_element_type=jnp.float32)
    mean = jnp.mean(embed, axis=-1, keepdims=True)
    centred = embed - mean
    variance = jnp.mean(centred * centred, axis=-1, keepdims=True)
    normed = (centred * lax.rsqrt(variance + 1e-06) * norm_gain + norm_bias).astype(jnp.bfloat16)
    normed = normed.reshape(pairs_here, rows_here, cols_all, channels)
    items = normed.reshape(pairs_here, rows_here, cols_all // 2, 2, channels)
    items = items.transpose(0, 2, 1, 3, 4).reshape(
        pairs_here * (cols_all // 2), rows_here, 2, channels
    )
    moved = lax.all_to_all(items, "tp", split_axis=0, concat_axis=1, tiled=True)
    owned = moved.shape[0]
    rows_full = moved.shape[1]
    merged = moved.reshape(owned, rows_full // 2, 2, 2, channels).reshape(
        owned * (rows_full // 2), 4 * channels
    )
    pre = (
        jnp.dot(
            lax.all_gather(merged, "tp", axis=0, tiled=True),
            proj_in,
            preferred_element_type=jnp.float32,
        )
        + bias_in
    )
    hidden = jax.nn.gelu(pre, approximate=False).astype(jnp.bfloat16)
    out_cols = proj_out.shape[1]
    summed = jnp.dot(
        lax.all_gather(hidden, "tp", axis=1, tiled=True),
        proj_out,
        preferred_element_type=jnp.float32,
    )
    result = (summed + bias_out).astype(jnp.bfloat16)
    result = result.reshape(pairs_here, cols_all // 2, rows_full // 2, out_cols).transpose(
        0, 2, 1, 3
    )
    return result


def per_device_whole_blocks(pixels, conv_weight, norm_gain, norm_bias, proj_in, bias_in, proj_out, bias_out):
    kernel = lax.all_gather(conv_weight, "tm", axis=1, tiled=True)
    pairs_here, rows_here, cols_all, patch_len = pixels.shape
    channels = kernel.shape[1]
    embed = jnp.dot(pixels.reshape(-1, patch_len), kernel, preferred_element_type=jnp.float32)
    mean = jnp.mean(embed, axis=-1, keepdims=True)
    centred = embed - mean
    variance = jnp.mean(centred * centred, axis=-1, keepdims=True)
    normed = (centred * lax.rsqrt(variance + 1e-06) * norm_gain + norm_bias).astype(jnp.bfloat16)
    normed = normed.reshape(pairs_here, rows_here, cols_all, channels)
    merged = normed.reshape(pairs_here, rows_here // 2, 2, cols_all // 2, 2, channels)
    merged = merged.transpose(0, 1, 3, 2, 4, 5).reshape(-1, 4 * channels)
    pre = (
        jnp.dot(
            lax.all_gather(merged, "tp", axis=0, tiled=True),
            proj_in,
            preferred_element_type=jnp.float32,
        )
        + bias_in
    )
    hidden = jax.nn.gelu(pre, approximate=False).astype(jnp.bfloat16)
    out_cols = proj_out.shape[1]
    summed = jnp.dot(
        lax.all_gather(hidden, "tp", axis=1, tiled=True),
        proj_out,
        preferred_element_type=jnp.float32,
    )
    result = (summed + bias_out).astype(jnp.bfloat16)
    tp = lax.axis_size("tp")
    result = result.reshape(tp, pairs_here, rows_here // 2, cols_all // 2, out_cols)
    result = result.transpose(1, 0, 2, 3, 4).reshape(
        pairs_here, tp * (rows_here // 2), cols_all // 2, out_cols
    )
    return result


MESH = pl.DeviceIdType.MESH
EPS = 1e-06
VMEM_BYTES = 60 * 1024 * 1024


def fused_kernel(
    dims,
    raw_ref, shard_ref, gain_ref, shift_ref, bias_in_ref, bias_out_ref, proj_in_ref, proj_out_ref,
    out_ref,
    x_ref, xs, turned, kernel, lhs, embed, merged, hidden, win, wout,
    own_sems, weight_sems,
    conv_send, conv_recv, conv_fwd_send, conv_fwd_recv,
    x_send, x_recv, m_send, m_recv,
    h_send, h_recv, h_own_send, h_own_recv, h_fwd_send, h_fwd_recv,
):
    tm_n, tp_n, pairs, bands, cols, main, rem, channels = dims
    line_n = tp_n // 2
    blocks = pairs * bands
    line_rows = line_n * cols
    hid_local = proj_in_ref.shape[1]
    share = shard_ref.shape[0]
    half = share // 2
    tm = lax.axis_index("tm")
    tp = lax.axis_index("tp")
    core = lax.rem(tp, 2)
    z = tp // 2
    sibling = (tm, z * 2 + 1 - core)

    def on_line(place):
        return (tm, place * 2 + core)

    last = line_n - 1
    inner = (z > 0) & (z < last)
    far_source = (2 - z) * last
    far_target = (z - 1) * last

    def each_reach(act):
        for e in (2, -2, 1, -1):
            place = z + e
            pl.when((place >= 0) & (place <= last))(functools.partial(act, place))

    def each_source(act):
        for place in range(line_n):
            pl.when(z != place)(functools.partial(act, place))

    def along_tm(d):
        return (lax.rem(tm + d, tm_n), tp)

    def remote(src, dst, send, recv, device):
        return pltpu.make_async_remote_copy(
            src_ref=src, dst_ref=dst, send_sem=send, recv_sem=recv, device_id=device, device_id_type=MESH
        )

    barrier = pltpu.get_barrier_semaphore()
    peers = [sibling]
    peers += [on_line(lax.rem(z + d, line_n)) for d in range(1, line_n)]
    peers += [along_tm(d) for d in range(1, tm_n)]
    for peer in peers:
        pl.semaphore_signal(barrier, inc=1, device_id=peer, device_id_type=MESH)

    weights = pltpu.make_async_copy(proj_in_ref, win, weight_sems.at[0])
    weights_out = pltpu.make_async_copy(proj_out_ref, wout, weight_sems.at[1])
    own_shard = pltpu.make_async_copy(
        shard_ref, turned.at[pl.ds(pl.multiple_of(tm * share, 16), share)], own_sems.at[0]
    )
    for copy in (own_shard, weights, weights_out):
        copy.start()

    lane = lax.broadcasted_iota(jnp.int32, (cols, 128), 1)
    for s in range(blocks):
        tail = jnp.zeros((cols, 128), jnp.float32)
        for g in range(4):
            rows = slice(g * cols, (g + 1) * cols)
            x_ref[s, :, g * main : (g + 1) * main] = raw_ref[s, rows, :main]
            end = raw_ref[s, rows, main:].astype(jnp.float32)
            end = jnp.concatenate([end, jnp.zeros((cols, 128 - rem), jnp.float32)], axis=1)
            tail += pltpu.roll(end, g * rem, 1) if g else end
        x_ref[s, :, 4 * main :] = tail.astype(jnp.bfloat16)
    own_blocks = [
        pltpu.make_async_copy(
            x_ref.at[s], xs.at[s, pl.ds(pl.multiple_of(z * cols, cols), cols)], own_sems.at[1 + s]
        )
        for s in range(blocks)
    ]
    for copy in own_blocks:
        copy.start()

    pl.semaphore_wait(barrier, len(peers))

    def shard_part(owner, which):
        return turned.at[pl.ds(pl.multiple_of(owner * share + which * half, 16), half)]

    conv = [
        remote(
            shard_ref.at[pl.ds(pl.multiple_of(core * half, 16), half)],
            shard_part(tm, core), conv_send.at[d - 1], conv_recv.at[d - 1], along_tm(d),
        )
        for d in range(1, tm_n)
    ]

    def x_part(s, place):
        return xs.at[s, pl.ds(pl.multiple_of(place * cols, cols), cols)]

    def x_copy(s, place):
        return remote(
            x_ref.at[s], x_part(s, z), x_send.at[s, place], x_recv.at[s, z], on_line(place)
        )

    def x_arrival(s, place):
        return remote(x_part(s, place), x_part(s, place), x_send.at[s, place], x_recv.at[s, place], sibling)

    def x_pass_on(s):
        part = x_part(s, far_source)
        return remote(part, part, x_send.at[s, z], x_recv.at[s, far_source], on_line(far_target))

    def pass_on_pixels(s):
        @pl.when(inner)
        def _():
            x_arrival(s, far_source).wait_recv()
            x_pass_on(s).start()

    for s in range(blocks):
        each_reach(lambda place, s=s: x_copy(s, place).start())
        for copy in conv[s : s + 1]:
            copy.start()
    for copy in conv[blocks:]:
        copy.start()
    pass_on_pixels(0)

    forwards = []
    for d in range(1, tm_n):
        part = shard_part(lax.rem(tm - d + tm_n, tm_n), core)
        remote(part, part, conv_send.at[d - 1], conv_recv.at[d - 1], sibling).wait_recv()
        copy = remote(part, part, conv_fwd_send.at[d - 1], conv_fwd_recv.at[d - 1], sibling)
        copy.start()
        forwards.append(copy)
    own_shard.wait()
    for d in range(1, tm_n):
        part = shard_part(lax.rem(tm - d + tm_n, tm_n), 1 - core)
        remote(part, part, conv_fwd_send.at[d - 1], conv_fwd_recv.at[d - 1], sibling).wait_recv()
    for copy in own_blocks:
        copy.wait()
    kernel[...] = turned[...].T
    weights.wait()
    pass_on_pixels(1)

    mine = pl.ds(pl.multiple_of(core * line_rows, line_rows), line_rows)
    other = pl.ds(pl.multiple_of((1 - core) * line_rows, line_rows), line_rows)
    hid_at = pl.multiple_of(tp * hid_local, 128)

    def h_part(s, owner):
        return hidden.at[s, :, pl.ds(pl.multiple_of(owner * hid_local, 128), hid_local)]

    def h_copy(s, place):
        return remote(h_part(s, tp), h_part(s, tp), h_send.at[s, place], h_recv.at[s, z], on_line(place))

    def h_arrival(s, place):
        part = h_part(s, place * 2 + core)
        return remote(part, part, h_send.at[s, place], h_recv.at[s, place], sibling)

    def h_pass_on(s):
        part = h_part(s, far_source * 2 + core)
        return remote(part, part, h_send.at[s, z], h_recv.at[s, far_source], on_line(far_target))

    def h_across(s, place, which):
        part = h_part(s, place * 2 + which)
        return remote(part, part, h_fwd_send.at[s, place], h_fwd_recv.at[s, place], sibling)

    def first_half(s, carry):
        def arrived(place):
            pl.when(jnp.logical_not(inner & (far_source == place)))(lambda: x_arrival(s, place).wait_recv())

        each_source(arrived)
        tail = xs[s, :, 4 * main :].astype(jnp.float32)
        for g in range(4):
            rows = slice(g * line_rows, (g + 1) * line_rows)
            lhs[rows, :main] = xs[s, :, g * main : (g + 1) * main]
            end = pltpu.roll(tail, 128 - g * rem, 1) if g else tail
            lhs[rows, main:] = end[:, :rem].astype(jnp.bfloat16)
        for n in range(0, channels, 256):
            part = jnp.dot(lhs[...], kernel[:, n : n + 256], preferred_element_type=jnp.float32)
            embed[n // 128] = part[:, :128]
            embed[n // 128 + 1] = part[:, 128:]
        part_rows = line_rows // 2
        for i in range(2):
            for j in range(2):
                for h in range(2):
                    every = pl.ds((2 * i + h) * line_rows + j, part_rows, stride=2)
                    value = jnp.concatenate([embed[k, every, :] for k in range(channels // 128)], axis=1)
                    mean = jnp.sum(value, axis=1, keepdims=True) * (1.0 / channels)
                    centred = value - mean
                    variance = jnp.sum(centred * centred, axis=1, keepdims=True) * (1.0 / channels)
                    normed = centred * lax.rsqrt(variance + EPS) * gain_ref[...] + shift_ref[...]
                    at = pl.ds(pl.multiple_of(core * line_rows + h * part_rows, part_rows), part_rows)
                    q = 2 * i + j
                    merged[s, at, q * channels : (q + 1) * channels] = normed.astype(jnp.bfloat16)
        to_sibling = remote(merged.at[s, mine], merged.at[s, mine], m_send.at[s], m_recv.at[s], sibling)
        to_sibling.start()
        remote(merged.at[s, other], merged.at[s, other], m_send.at[s], m_recv.at[s], sibling).wait_recv()
        pre = jnp.dot(merged[s], win[...], preferred_element_type=jnp.float32) + bias_in_ref[...]
        act = 0.5 * pre * (1.0 + lax.erf(pre * (0.5**0.5)))
        hidden[s, :, pl.ds(hid_at, hid_local)] = act.astype(jnp.bfloat16)
        each_reach(lambda place: h_copy(s, place).start())
        remote(h_part(s, tp), h_part(s, tp), h_own_send.at[s], h_own_recv.at[s], sibling).start()
        pl.when(s + 2 < blocks)(lambda: pass_on_pixels(s + 2))
        return carry

    lax.fori_loop(0, blocks, first_half, 0)
    weights_out.wait()

    def hand_over(s):
        @pl.when(inner)
        def _():
            h_arrival(s, far_source).wait_recv()
            h_pass_on(s).start()
            h_across(s, far_source, core).start()

        def arrived(place):
            @pl.when(jnp.logical_not(inner & (far_source == place)))
            def _():
                h_arrival(s, place).wait_recv()
                h_across(s, place, core).start()

        each_source(arrived)

    def second_half(s):
        part = h_part(s, z * 2 + 1 - core)
        remote(part, part, h_own_send.at[s], h_own_recv.at[s], sibling).wait_recv()
        each_source(lambda place: h_across(s, place, 1 - core).wait_recv())
        pair, band = s // bands, lax.rem(s, bands)
        for n in range(0, out_ref.shape[1], 256):
            total = jnp.dot(hidden[s], wout[:, n : n + 256], preferred_element_type=jnp.float32)
            result = total + bias_out_ref[:, n : n + 256]
            for c in range(2):
                for l in range(line_n):
                    at = ((pair * tp_n + l * 2 + c) * bands + band) * cols
                    low = c * line_rows + l * (cols // 2)
                    high = low + line_rows // 2
                    tokens = [result[low : low + cols // 2], result[high : high + cols // 2]]
                    tokens = jnp.concatenate(tokens, axis=0).astype(jnp.bfloat16)
                    out_ref[pl.ds(pl.multiple_of(at, cols), cols), n : n + 256] = tokens

    hand_over(0)

    def finish(s, carry):
        hand_over(s)
        second_half(s - 1)
        return carry

    lax.fori_loop(1, blocks, finish, 0)
    second_half(blocks - 1)

    for copy in conv + forwards:
        copy.wait_send()

    def drain(s, carry):
        remote(merged.at[s, mine], merged.at[s, mine], m_send.at[s], m_recv.at[s], sibling).wait_send()
        remote(h_part(s, tp), h_part(s, tp), h_own_send.at[s], h_own_recv.at[s], sibling).wait_send()
        each_reach(lambda place: x_copy(s, place).wait_send())
        each_reach(lambda place: h_copy(s, place).wait_send())
        each_source(lambda place: h_across(s, place, core).wait_send())

        @pl.when(inner)
        def _():
            x_pass_on(s).wait_send()
            h_pass_on(s).wait_send()

        return carry

    lax.fori_loop(0, blocks, drain, 0)


def per_device_fused(pixels, conv_weight, norm_gain, norm_bias, proj_in, bias_in, proj_out, bias_out):
    tm_n, tp_n = lax.axis_size("tm"), lax.axis_size("tp")
    pairs, rows, grid_cols, patch = pixels.shape
    channels = conv_weight.shape[1] * tm_n
    bands, cols = rows // 2, grid_cols // 2
    main = patch // 128 * 128
    rem = patch - main
    blocks = pairs * bands
    line_n = tp_n // 2
    group = tp_n * cols
    bf16 = jnp.bfloat16
    dma = pltpu.SemaphoreType.DMA
    vmem = pl.BlockSpec(memory_space=pltpu.VMEM)
    anywhere = pl.BlockSpec(memory_space=pl.ANY)
    conv_sems = [dma((tm_n - 1,))] * 4
    packed = 4 * main + 128
    line_sems = dma((blocks, line_n))
    out = pl.pallas_call(
        functools.partial(fused_kernel, (tm_n, tp_n, pairs, bands, cols, main, rem, channels)),
        out_shape=jax.ShapeDtypeStruct((blocks * group, proj_out.shape[1]), bf16),
        in_specs=[vmem] * 6 + [anywhere] * 2,
        out_specs=vmem,
        scratch_shapes=[
            pltpu.VMEM((blocks, cols, packed), bf16),
            pltpu.VMEM((blocks, line_n * cols, packed), bf16),
            pltpu.VMEM((channels, patch), bf16),
            pltpu.VMEM((patch, channels), bf16),
            pltpu.VMEM((4 * line_n * cols, patch), bf16),
            pltpu.VMEM((channels // 128, 4 * line_n * cols, 128), jnp.float32),
            pltpu.VMEM((blocks, group, 4 * channels), bf16),
            pltpu.VMEM((blocks, group, proj_out.shape[0]), bf16),
            pltpu.VMEM(proj_in.shape, bf16),
            pltpu.VMEM(proj_out.shape, bf16),
            dma((1 + blocks,)),
            dma((2,)),
        ]
        + conv_sems
        + [line_sems] * 2
        + [dma((blocks,))] * 2
        + [line_sems] * 2
        + [dma((blocks,))] * 2
        + [line_sems] * 2,
        compiler_params=pltpu.CompilerParams(
            collective_id=0, has_side_effects=True, vmem_limit_bytes=VMEM_BYTES
        ),
    )(
        pixels.reshape(blocks, 2 * grid_cols, patch), conv_weight.T,
        norm_gain.reshape(1, -1), norm_bias.reshape(1, -1),
        bias_in.reshape(1, -1), bias_out.reshape(1, -1), proj_in, proj_out,
    )
    return out.reshape(pairs, tp_n * bands, cols, proj_out.shape[1])


def fused_fits(pixels, conv_weight, proj_in, proj_out):
    pairs, rows, grid_cols, patch = pixels.shape
    tm_n, tp_n = lax.axis_size("tm"), lax.axis_size("tp")
    local = conv_weight.shape[1]
    held = 2 * (proj_in.size + proj_out.size) + 8 * pairs * tp_n * rows * grid_cols * local * tm_n // 2
    return (
        rows % 2 == 0
        and grid_cols % 32 == 0
        and tm_n >= 2
        and tp_n % 2 == 0
        and tp_n == 8
        and pairs * rows >= 4
        and local % 32 == 0
        and local * tm_n % 256 == 0
        and patch % 128 != 0
        and 4 * (patch % 128) <= 128
        and proj_in.shape[1] % 128 == 0
        and proj_out.shape[1] % 256 == 0
        and held < VMEM_BYTES // 3 * 2
    )


def per_device(pixels, conv_weight, norm_gain, norm_bias, proj_in, bias_in, proj_out, bias_out):
    if fused_fits(pixels, conv_weight, proj_in, proj_out):
        body = per_device_fused
    elif pixels.shape[1] % 2 == 0:
        body = per_device_whole_blocks
    else:
        body = per_device_split_blocks
    return body(pixels, conv_weight, norm_gain, norm_bias, proj_in, bias_in, proj_out, bias_out)


def solution(mesh):
    return jax.shard_map(
        per_device,
        mesh=mesh,
        in_specs=(
            P("tm", "tp", None, None),
            P(None, "tm"),
            P(),
            P(),
            P(None, "tp"),
            P("tp"),
            P(None, "tp"),
            P("tp"),
        ),
        out_specs=P("tm", None, None, "tp"),
        check_vma=False,
    )
```

```python
import functools

import jax
import jax.numpy as jnp
from jax import lax
from jax.experimental import pallas as pl
from jax.experimental.pallas import tpu as pltpu
from jax.sharding import PartitionSpec as P


def per_device_split_blocks(pixels, conv_weight, norm_gain, norm_bias, proj_in, bias_in, proj_out, bias_out):
    kernel = lax.all_gather(conv_weight, "tm", axis=1, tiled=True)
    pairs_here, rows_here, cols_all, patch_len = pixels.shape
    channels = kernel.shape[1]
    embed = jnp.dot(pixels.reshape(-1, patch_len), kernel, preferred_element_type=jnp.float32)
    mean = jnp.mean(embed, axis=-1, keepdims=True)
    centred = embed - mean
    variance = jnp.mean(centred * centred, axis=-1, keepdims=True)
    normed = (centred * lax.rsqrt(variance + 1e-06) * norm_gain + norm_bias).astype(jnp.bfloat16)
    normed = normed.reshape(pairs_here, rows_here, cols_all, channels)
    items = normed.reshape(pairs_here, rows_here, cols_all // 2, 2, channels)
    items = items.transpose(0, 2, 1, 3, 4).reshape(
        pairs_here * (cols_all // 2), rows_here, 2, channels
    )
    moved = lax.all_to_all(items, "tp", split_axis=0, concat_axis=1, tiled=True)
    owned = moved.shape[0]
    rows_full = moved.shape[1]
    merged = moved.reshape(owned, rows_full // 2, 2, 2, channels).reshape(
        owned * (rows_full // 2), 4 * channels
    )
    pre = (
        jnp.dot(
            lax.all_gather(merged, "tp", axis=0, tiled=True),
            proj_in,
            preferred_element_type=jnp.float32,
        )
        + bias_in
    )
    hidden = jax.nn.gelu(pre, approximate=False).astype(jnp.bfloat16)
    out_cols = proj_out.shape[1]
    summed = jnp.dot(
        lax.all_gather(hidden, "tp", axis=1, tiled=True),
        proj_out,
        preferred_element_type=jnp.float32,
    )
    result = (summed + bias_out).astype(jnp.bfloat16)
    result = result.reshape(pairs_here, cols_all // 2, rows_full // 2, out_cols).transpose(
        0, 2, 1, 3
    )
    return result


def per_device_whole_blocks(pixels, conv_weight, norm_gain, norm_bias, proj_in, bias_in, proj_out, bias_out):
    kernel = lax.all_gather(conv_weight, "tm", axis=1, tiled=True)
    pairs_here, rows_here, cols_all, patch_len = pixels.shape
    channels = kernel.shape[1]
    embed = jnp.dot(pixels.reshape(-1, patch_len), kernel, preferred_element_type=jnp.float32)
    mean = jnp.mean(embed, axis=-1, keepdims=True)
    centred = embed - mean
    variance = jnp.mean(centred * centred, axis=-1, keepdims=True)
    normed = (centred * lax.rsqrt(variance + 1e-06) * norm_gain + norm_bias).astype(jnp.bfloat16)
    normed = normed.reshape(pairs_here, rows_here, cols_all, channels)
    merged = normed.reshape(pairs_here, rows_here // 2, 2, cols_all // 2, 2, channels)
    merged = merged.transpose(0, 1, 3, 2, 4, 5).reshape(-1, 4 * channels)
    pre = (
        jnp.dot(
            lax.all_gather(merged, "tp", axis=0, tiled=True),
            proj_in,
            preferred_element_type=jnp.float32,
        )
        + bias_in
    )
    hidden = jax.nn.gelu(pre, approximate=False).astype(jnp.bfloat16)
    out_cols = proj_out.shape[1]
    summed = jnp.dot(
        lax.all_gather(hidden, "tp", axis=1, tiled=True),
        proj_out,
        preferred_element_type=jnp.float32,
    )
    result = (summed + bias_out).astype(jnp.bfloat16)
    tp = lax.axis_size("tp")
    result = result.reshape(tp, pairs_here, rows_here // 2, cols_all // 2, out_cols)
    result = result.transpose(1, 0, 2, 3, 4).reshape(
        pairs_here, tp * (rows_here // 2), cols_all // 2, out_cols
    )
    return result


MESH = pl.DeviceIdType.MESH
EPS = 1e-06
VMEM_BYTES = 60 * 1024 * 1024


def fused_kernel(
    dims,
    raw_ref, shard_ref, gain_ref, shift_ref, bias_in_ref, bias_out_ref, proj_in_ref, proj_out_ref,
    out_ref,
    x_ref, xs, turned, kernel, lhs, embed, merged, hidden, win, wout,
    own_sems, weight_sems,
    conv_send, conv_recv, conv_fwd_send, conv_fwd_recv,
    x_send, x_recv, m_send, m_recv,
    h_send, h_recv, h_own_send, h_own_recv, h_fwd_send, h_fwd_recv,
):
    tm_n, tp_n, pairs, bands, cols, main, rem, channels = dims
    line_n = tp_n // 2
    blocks = pairs * bands
    line_rows = line_n * cols
    hid_local = proj_in_ref.shape[1]
    share = shard_ref.shape[0]
    half = share // 2
    tm = lax.axis_index("tm")
    tp = lax.axis_index("tp")
    core = lax.rem(tp, 2)
    z = tp // 2
    sibling = (tm, z * 2 + 1 - core)

    def on_line(place):
        return (tm, place * 2 + core)

    last = line_n - 1
    inner = (z > 0) & (z < last)
    far_source = (2 - z) * last
    far_target = (z - 1) * last

    def each_reach(act):
        for e in (2, -2, 1, -1):
            place = z + e
            pl.when((place >= 0) & (place <= last))(functools.partial(act, place))

    def each_source(act):
        for place in range(line_n):
            pl.when(z != place)(functools.partial(act, place))

    def along_tm(d):
        return (lax.rem(tm + d, tm_n), tp)

    def remote(src, dst, send, recv, device):
        return pltpu.make_async_remote_copy(
            src_ref=src, dst_ref=dst, send_sem=send, recv_sem=recv, device_id=device, device_id_type=MESH
        )

    barrier = pltpu.get_barrier_semaphore()
    peers = [sibling]
    peers += [on_line(lax.rem(z + d, line_n)) for d in range(1, line_n)]
    peers += [along_tm(d) for d in range(1, tm_n)]
    for peer in peers:
        pl.semaphore_signal(barrier, inc=1, device_id=peer, device_id_type=MESH)

    weights = pltpu.make_async_copy(proj_in_ref, win, weight_sems.at[0])
    weights_out = pltpu.make_async_copy(proj_out_ref, wout, weight_sems.at[1])
    own_shard = pltpu.make_async_copy(
        shard_ref, turned.at[pl.ds(pl.multiple_of(tm * share, 16), share)], own_sems.at[0]
    )
    for copy in (own_shard, weights, weights_out):
        copy.start()

    lane = lax.broadcasted_iota(jnp.int32, (cols, 128), 1)
    for s in range(blocks):
        tail = jnp.zeros((cols, 128), jnp.float32)
        for g in range(4):
            rows = slice(g * cols, (g + 1) * cols)
            x_ref[s, :, g * main : (g + 1) * main] = raw_ref[s, rows, :main]
            end = raw_ref[s, rows, main:].astype(jnp.float32)
            end = jnp.concatenate([end, jnp.zeros((cols, 128 - rem), jnp.float32)], axis=1)
            tail += pltpu.roll(end, g * rem, 1) if g else end
        x_ref[s, :, 4 * main :] = tail.astype(jnp.bfloat16)
    own_blocks = [
        pltpu.make_async_copy(
            x_ref.at[s], xs.at[s, pl.ds(pl.multiple_of(z * cols, cols), cols)], own_sems.at[1 + s]
        )
        for s in range(blocks)
    ]
    for copy in own_blocks:
        copy.start()

    pl.semaphore_wait(barrier, len(peers))

    def shard_part(owner, which):
        return turned.at[pl.ds(pl.multiple_of(owner * share + which * half, 16), half)]

    conv = [
        remote(
            shard_ref.at[pl.ds(pl.multiple_of(core * half, 16), half)],
            shard_part(tm, core), conv_send.at[d - 1], conv_recv.at[d - 1], along_tm(d),
        )
        for d in range(1, tm_n)
    ]

    def x_part(s, place):
        return xs.at[s, pl.ds(pl.multiple_of(place * cols, cols), cols)]

    def x_copy(s, place):
        return remote(
            x_ref.at[s], x_part(s, z), x_send.at[s, place], x_recv.at[s, z], on_line(place)
        )

    def x_arrival(s, place):
        return remote(x_part(s, place), x_part(s, place), x_send.at[s, place], x_recv.at[s, place], sibling)

    def x_pass_on(s):
        part = x_part(s, far_source)
        return remote(part, part, x_send.at[s, z], x_recv.at[s, far_source], on_line(far_target))

    def pass_on_pixels(s):
        @pl.when(inner)
        def _():
            x_arrival(s, far_source).wait_recv()
            x_pass_on(s).start()

    for s in range(blocks):
        each_reach(lambda place, s=s: x_copy(s, place).start())
        for copy in conv[s : s + 1]:
            copy.start()
    for copy in conv[blocks:]:
        copy.start()
    pass_on_pixels(0)

    forwards = []
    for d in range(1, tm_n):
        part = shard_part(lax.rem(tm - d + tm_n, tm_n), core)
        remote(part, part, conv_send.at[d - 1], conv_recv.at[d - 1], sibling).wait_recv()
        copy = remote(part, part, conv_fwd_send.at[d - 1], conv_fwd_recv.at[d - 1], sibling)
        copy.start()
        forwards.append(copy)
    own_shard.wait()
    for d in range(1, tm_n):
        part = shard_part(lax.rem(tm - d + tm_n, tm_n), 1 - core)
        remote(part, part, conv_fwd_send.at[d - 1], conv_fwd_recv.at[d - 1], sibling).wait_recv()
    for copy in own_blocks:
        copy.wait()
    kernel[...] = turned[...].T
    weights.wait()
    pass_on_pixels(1)

    mine = pl.ds(pl.multiple_of(core * line_rows, line_rows), line_rows)
    other = pl.ds(pl.multiple_of((1 - core) * line_rows, line_rows), line_rows)
    hid_at = pl.multiple_of(tp * hid_local, 128)

    def h_part(s, owner):
        return hidden.at[s, :, pl.ds(pl.multiple_of(owner * hid_local, 128), hid_local)]

    def h_copy(s, place):
        return remote(h_part(s, tp), h_part(s, tp), h_send.at[s, place], h_recv.at[s, z], on_line(place))

    def h_arrival(s, place):
        part = h_part(s, place * 2 + core)
        return remote(part, part, h_send.at[s, place], h_recv.at[s, place], sibling)

    def h_pass_on(s):
        part = h_part(s, far_source * 2 + core)
        return remote(part, part, h_send.at[s, z], h_recv.at[s, far_source], on_line(far_target))

    def h_across(s, place, which):
        part = h_part(s, place * 2 + which)
        return remote(part, part, h_fwd_send.at[s, place], h_fwd_recv.at[s, place], sibling)

    def pass_on_hidden(s):
        @pl.when(inner)
        def _():
            h_arrival(s, far_source).wait_recv()
            h_pass_on(s).start()

    gain, shift = gain_ref[...].reshape(1, -1), shift_ref[...].reshape(1, -1)
    bias_in, bias_out = bias_in_ref[...].reshape(1, -1), bias_out_ref[...].reshape(1, -1)

    def embed_block(s):
        def arrived(place):
            pl.when(jnp.logical_not(inner & (far_source == place)))(lambda: x_arrival(s, place).wait_recv())

        each_source(arrived)
        tail = xs[s, :, 4 * main :].astype(jnp.float32)
        for g in range(4):
            rows = slice(g * line_rows, (g + 1) * line_rows)
            lhs[rows, :main] = xs[s, :, g * main : (g + 1) * main]
            end = pltpu.roll(tail, 128 - g * rem, 1) if g else tail
            lhs[rows, main:] = end[:, :rem].astype(jnp.bfloat16)
        for n in range(0, channels, 256):
            part = jnp.dot(lhs[...], kernel[:, n : n + 256], preferred_element_type=jnp.float32)
            embed[n // 128] = part[:, :128]
            embed[n // 128 + 1] = part[:, 128:]
        part_rows = line_rows // 2
        for i in range(2):
            for j in range(2):
                for h in range(2):
                    every = pl.ds((2 * i + h) * line_rows + j, part_rows, stride=2)
                    value = jnp.concatenate([embed[k, every, :] for k in range(channels // 128)], axis=1)
                    mean = jnp.sum(value, axis=1, keepdims=True) * (1.0 / channels)
                    centred = value - mean
                    variance = jnp.sum(centred * centred, axis=1, keepdims=True) * (1.0 / channels)
                    normed = centred * lax.rsqrt(variance + EPS) * gain + shift
                    at = pl.ds(pl.multiple_of(core * line_rows + h * part_rows, part_rows), part_rows)
                    q = 2 * i + j
                    merged[s, at, q * channels : (q + 1) * channels] = normed.astype(jnp.bfloat16)
        to_sibling = remote(merged.at[s, mine], merged.at[s, mine], m_send.at[s], m_recv.at[s], sibling)
        to_sibling.start()

    def hidden_block(s):
        remote(merged.at[s, other], merged.at[s, other], m_send.at[s], m_recv.at[s], sibling).wait_recv()
        pre = jnp.dot(merged[s], win[...], preferred_element_type=jnp.float32) + bias_in
        act = 0.5 * pre * (1.0 + lax.erf(pre * (0.5**0.5)))
        hidden[s, :, pl.ds(hid_at, hid_local)] = act.astype(jnp.bfloat16)
        each_reach(lambda place: h_copy(s, place).start())
        remote(h_part(s, tp), h_part(s, tp), h_own_send.at[s], h_own_recv.at[s], sibling).start()

    def first_half(s, carry):
        pl.when(s < blocks)(lambda: embed_block(s))
        pl.when(s + 2 < blocks)(lambda: pass_on_pixels(s + 2))
        pl.when(s > 0)(lambda: hidden_block(s - 1))
        pl.when(s > 2)(lambda: pass_on_hidden(s - 3))
        return carry

    lax.fori_loop(0, blocks + 1, first_half, 0)
    weights_out.wait()

    def hand_over(s):
        pl.when(s >= blocks - 2)(lambda: pass_on_hidden(s))
        pl.when(inner)(lambda: h_across(s, far_source, core).start())

        def arrived(place):
            @pl.when(jnp.logical_not(inner & (far_source == place)))
            def _():
                h_arrival(s, place).wait_recv()
                h_across(s, place, core).start()

        each_source(arrived)

    def second_half(s):
        part = h_part(s, z * 2 + 1 - core)
        remote(part, part, h_own_send.at[s], h_own_recv.at[s], sibling).wait_recv()
        each_source(lambda place: h_across(s, place, 1 - core).wait_recv())
        pair, band = s // bands, lax.rem(s, bands)
        for n in range(0, out_ref.shape[1], 256):
            total = jnp.dot(hidden[s], wout[:, n : n + 256], preferred_element_type=jnp.float32)
            result = total + bias_out[:, n : n + 256]
            for c in range(2):
                for l in range(line_n):
                    at = ((pair * tp_n + l * 2 + c) * bands + band) * cols
                    low = c * line_rows + l * (cols // 2)
                    high = low + line_rows // 2
                    tokens = [result[low : low + cols // 2], result[high : high + cols // 2]]
                    tokens = jnp.concatenate(tokens, axis=0).astype(jnp.bfloat16)
                    out_ref[pl.ds(pl.multiple_of(at, cols), cols), n : n + 256] = tokens

    hand_over(0)

    def finish(s, carry):
        hand_over(s)
        second_half(s - 1)
        return carry

    lax.fori_loop(1, blocks, finish, 0)
    second_half(blocks - 1)

    for copy in conv + forwards:
        copy.wait_send()

    def drain(s, carry):
        remote(merged.at[s, mine], merged.at[s, mine], m_send.at[s], m_recv.at[s], sibling).wait_send()
        remote(h_part(s, tp), h_part(s, tp), h_own_send.at[s], h_own_recv.at[s], sibling).wait_send()
        each_reach(lambda place: x_copy(s, place).wait_send())
        each_reach(lambda place: h_copy(s, place).wait_send())
        each_source(lambda place: h_across(s, place, core).wait_send())

        @pl.when(inner)
        def _():
            x_pass_on(s).wait_send()
            h_pass_on(s).wait_send()

        return carry

    lax.fori_loop(0, blocks, drain, 0)


def per_device_fused(pixels, conv_weight, norm_gain, norm_bias, proj_in, bias_in, proj_out, bias_out):
    tm_n, tp_n = lax.axis_size("tm"), lax.axis_size("tp")
    pairs, rows, grid_cols, patch = pixels.shape
    channels = conv_weight.shape[1] * tm_n
    bands, cols = rows // 2, grid_cols // 2
    main = patch // 128 * 128
    rem = patch - main
    blocks = pairs * bands
    line_n = tp_n // 2
    group = tp_n * cols
    bf16 = jnp.bfloat16
    dma = pltpu.SemaphoreType.DMA
    vmem = pl.BlockSpec(memory_space=pltpu.VMEM)
    anywhere = pl.BlockSpec(memory_space=pl.ANY)
    conv_sems = [dma((tm_n - 1,))] * 4
    packed = 4 * main + 128
    line_sems = dma((blocks, line_n))
    out = pl.pallas_call(
        functools.partial(fused_kernel, (tm_n, tp_n, pairs, bands, cols, main, rem, channels)),
        out_shape=jax.ShapeDtypeStruct((blocks * group, proj_out.shape[1]), bf16),
        in_specs=[vmem] * 6 + [anywhere] * 2,
        out_specs=vmem,
        scratch_shapes=[
            pltpu.VMEM((blocks, cols, packed), bf16),
            pltpu.VMEM((blocks, line_n * cols, packed), bf16),
            pltpu.VMEM((channels, patch), bf16),
            pltpu.VMEM((patch, channels), bf16),
            pltpu.VMEM((4 * line_n * cols, patch), bf16),
            pltpu.VMEM((channels // 128, 4 * line_n * cols, 128), jnp.float32),
            pltpu.VMEM((blocks, group, 4 * channels), bf16),
            pltpu.VMEM((blocks, group, proj_out.shape[0]), bf16),
            pltpu.VMEM(proj_in.shape, bf16),
            pltpu.VMEM(proj_out.shape, bf16),
            dma((1 + blocks,)),
            dma((2,)),
        ]
        + conv_sems
        + [line_sems] * 2
        + [dma((blocks,))] * 2
        + [line_sems] * 2
        + [dma((blocks,))] * 2
        + [line_sems] * 2,
        compiler_params=pltpu.CompilerParams(
            collective_id=0, has_side_effects=True, vmem_limit_bytes=VMEM_BYTES
        ),
    )(
        pixels.reshape(blocks, 2 * grid_cols, patch), conv_weight.T,
        norm_gain, norm_bias, bias_in, bias_out, proj_in, proj_out,
    )
    return out.reshape(pairs, tp_n * bands, cols, proj_out.shape[1])


def fused_fits(pixels, conv_weight, proj_in, proj_out):
    pairs, rows, grid_cols, patch = pixels.shape
    tm_n, tp_n = lax.axis_size("tm"), lax.axis_size("tp")
    local = conv_weight.shape[1]
    held = 2 * (proj_in.size + proj_out.size) + 8 * pairs * tp_n * rows * grid_cols * local * tm_n // 2
    return (
        rows % 2 == 0
        and grid_cols % 32 == 0
        and tm_n >= 2
        and tp_n % 2 == 0
        and tp_n == 8
        and pairs * rows >= 4
        and local % 32 == 0
        and local * tm_n % 256 == 0
        and patch % 128 != 0
        and 4 * (patch % 128) <= 128
        and proj_in.shape[1] % 128 == 0
        and proj_out.shape[1] % 256 == 0
        and held < VMEM_BYTES // 3 * 2
    )


def per_device(pixels, conv_weight, norm_gain, norm_bias, proj_in, bias_in, proj_out, bias_out):
    if fused_fits(pixels, conv_weight, proj_in, proj_out):
        body = per_device_fused
    elif pixels.shape[1] % 2 == 0:
        body = per_device_whole_blocks
    else:
        body = per_device_split_blocks
    return body(pixels, conv_weight, norm_gain, norm_bias, proj_in, bias_in, proj_out, bias_out)


def solution(mesh):
    return jax.shard_map(
        per_device,
        mesh=mesh,
        in_specs=(
            P("tm", "tp", None, None),
            P(None, "tm"),
            P(),
            P(),
            P(None, "tp"),
            P("tp"),
            P(None, "tp"),
            P("tp"),
        ),
        out_specs=P("tm", None, None, "tp"),
        check_vma=False,
    )
```

```python
import functools

import jax
import jax.numpy as jnp
from jax import lax
from jax.experimental import pallas as pl
from jax.experimental.pallas import tpu as pltpu
from jax.sharding import PartitionSpec as P


def per_device_split_blocks(pixels, conv_weight, norm_gain, norm_bias, proj_in, bias_in, proj_out, bias_out):
    kernel = lax.all_gather(conv_weight, "tm", axis=1, tiled=True)
    pairs_here, rows_here, cols_all, patch_len = pixels.shape
    channels = kernel.shape[1]
    embed = jnp.dot(pixels.reshape(-1, patch_len), kernel, preferred_element_type=jnp.float32)
    mean = jnp.mean(embed, axis=-1, keepdims=True)
    centred = embed - mean
    variance = jnp.mean(centred * centred, axis=-1, keepdims=True)
    normed = (centred * lax.rsqrt(variance + 1e-06) * norm_gain + norm_bias).astype(jnp.bfloat16)
    normed = normed.reshape(pairs_here, rows_here, cols_all, channels)
    items = normed.reshape(pairs_here, rows_here, cols_all // 2, 2, channels)
    items = items.transpose(0, 2, 1, 3, 4).reshape(
        pairs_here * (cols_all // 2), rows_here, 2, channels
    )
    moved = lax.all_to_all(items, "tp", split_axis=0, concat_axis=1, tiled=True)
    owned = moved.shape[0]
    rows_full = moved.shape[1]
    merged = moved.reshape(owned, rows_full // 2, 2, 2, channels).reshape(
        owned * (rows_full // 2), 4 * channels
    )
    pre = (
        jnp.dot(
            lax.all_gather(merged, "tp", axis=0, tiled=True),
            proj_in,
            preferred_element_type=jnp.float32,
        )
        + bias_in
    )
    hidden = jax.nn.gelu(pre, approximate=False).astype(jnp.bfloat16)
    out_cols = proj_out.shape[1]
    summed = jnp.dot(
        lax.all_gather(hidden, "tp", axis=1, tiled=True),
        proj_out,
        preferred_element_type=jnp.float32,
    )
    result = (summed + bias_out).astype(jnp.bfloat16)
    result = result.reshape(pairs_here, cols_all // 2, rows_full // 2, out_cols).transpose(
        0, 2, 1, 3
    )
    return result


def per_device_whole_blocks(pixels, conv_weight, norm_gain, norm_bias, proj_in, bias_in, proj_out, bias_out):
    kernel = lax.all_gather(conv_weight, "tm", axis=1, tiled=True)
    pairs_here, rows_here, cols_all, patch_len = pixels.shape
    channels = kernel.shape[1]
    embed = jnp.dot(pixels.reshape(-1, patch_len), kernel, preferred_element_type=jnp.float32)
    mean = jnp.mean(embed, axis=-1, keepdims=True)
    centred = embed - mean
    variance = jnp.mean(centred * centred, axis=-1, keepdims=True)
    normed = (centred * lax.rsqrt(variance + 1e-06) * norm_gain + norm_bias).astype(jnp.bfloat16)
    normed = normed.reshape(pairs_here, rows_here, cols_all, channels)
    merged = normed.reshape(pairs_here, rows_here // 2, 2, cols_all // 2, 2, channels)
    merged = merged.transpose(0, 1, 3, 2, 4, 5).reshape(-1, 4 * channels)
    pre = (
        jnp.dot(
            lax.all_gather(merged, "tp", axis=0, tiled=True),
            proj_in,
            preferred_element_type=jnp.float32,
        )
        + bias_in
    )
    hidden = jax.nn.gelu(pre, approximate=False).astype(jnp.bfloat16)
    out_cols = proj_out.shape[1]
    summed = jnp.dot(
        lax.all_gather(hidden, "tp", axis=1, tiled=True),
        proj_out,
        preferred_element_type=jnp.float32,
    )
    result = (summed + bias_out).astype(jnp.bfloat16)
    tp = lax.axis_size("tp")
    result = result.reshape(tp, pairs_here, rows_here // 2, cols_all // 2, out_cols)
    result = result.transpose(1, 0, 2, 3, 4).reshape(
        pairs_here, tp * (rows_here // 2), cols_all // 2, out_cols
    )
    return result


MESH = pl.DeviceIdType.MESH
EPS = 1e-06
VMEM_BYTES = 60 * 1024 * 1024


def fused_kernel(
    dims,
    raw_ref, shard_ref, gain_ref, shift_ref, bias_in_ref, bias_out_ref, proj_in_ref, proj_out_ref,
    out_ref,
    x_ref, xs, turned, kernel, lhs, embed, merged, hidden, win, wout,
    own_sems, weight_sems,
    conv_send, conv_recv, conv_fwd_send, conv_fwd_recv,
    x_send, x_recv, m_send, m_recv,
    h_send, h_recv, h_own_send, h_own_recv, h_fwd_send, h_fwd_recv,
):
    tm_n, tp_n, pairs, bands, cols, main, rem, channels = dims
    line_n = tp_n // 2
    blocks = pairs * bands
    line_rows = line_n * cols
    hid_local = proj_in_ref.shape[1]
    share = shard_ref.shape[0]
    half = share // 2
    tm = lax.axis_index("tm")
    tp = lax.axis_index("tp")
    core = lax.rem(tp, 2)
    z = tp // 2
    sibling = (tm, z * 2 + 1 - core)

    def on_line(place):
        return (tm, place * 2 + core)

    last = line_n - 1
    inner = (z > 0) & (z < last)
    far_source = (2 - z) * last
    far_target = (z - 1) * last

    def each_reach(act):
        for e in (2, -2, 1, -1):
            place = z + e
            pl.when((place >= 0) & (place <= last))(functools.partial(act, place))

    def each_source(act):
        for place in range(line_n):
            pl.when(z != place)(functools.partial(act, place))

    def along_tm(d):
        return (lax.rem(tm + d, tm_n), tp)

    def remote(src, dst, send, recv, device):
        return pltpu.make_async_remote_copy(
            src_ref=src, dst_ref=dst, send_sem=send, recv_sem=recv, device_id=device, device_id_type=MESH
        )

    barrier = pltpu.get_barrier_semaphore()
    peers = [sibling]
    peers += [on_line(lax.rem(z + d, line_n)) for d in range(1, line_n)]
    peers += [along_tm(d) for d in range(1, tm_n)]
    for peer in peers:
        pl.semaphore_signal(barrier, inc=1, device_id=peer, device_id_type=MESH)

    weights = pltpu.make_async_copy(proj_in_ref, win, weight_sems.at[0])
    weights_out = pltpu.make_async_copy(proj_out_ref, wout, weight_sems.at[1])
    own_shard = pltpu.make_async_copy(
        shard_ref, turned.at[pl.ds(pl.multiple_of(tm * share, 16), share)], own_sems.at[0]
    )
    for copy in (own_shard, weights, weights_out):
        copy.start()

    lane = lax.broadcasted_iota(jnp.int32, (cols, 128), 1)
    for s in range(blocks):
        tail = jnp.zeros((cols, 128), jnp.float32)
        for g in range(4):
            rows = slice(g * cols, (g + 1) * cols)
            x_ref[s, :, g * main : (g + 1) * main] = raw_ref[s, rows, :main]
            end = raw_ref[s, rows, main:].astype(jnp.float32)
            end = jnp.concatenate([end, jnp.zeros((cols, 128 - rem), jnp.float32)], axis=1)
            tail += pltpu.roll(end, g * rem, 1) if g else end
        x_ref[s, :, 4 * main :] = tail.astype(jnp.bfloat16)
    own_blocks = [
        pltpu.make_async_copy(
            x_ref.at[s], xs.at[s, pl.ds(pl.multiple_of(z * cols, cols), cols)], own_sems.at[1 + s]
        )
        for s in range(blocks)
    ]
    for copy in own_blocks:
        copy.start()

    pl.semaphore_wait(barrier, len(peers))

    def shard_part(owner, which):
        return turned.at[pl.ds(pl.multiple_of(owner * share + which * half, 16), half)]

    conv = [
        remote(
            shard_ref.at[pl.ds(pl.multiple_of(core * half, 16), half)],
            shard_part(tm, core), conv_send.at[d - 1], conv_recv.at[d - 1], along_tm(d),
        )
        for d in range(1, tm_n)
    ]

    def x_part(s, place):
        return xs.at[s, pl.ds(pl.multiple_of(place * cols, cols), cols)]

    def x_copy(s, place):
        return remote(
            x_ref.at[s], x_part(s, z), x_send.at[s, place], x_recv.at[s, z], on_line(place)
        )

    def x_arrival(s, place):
        return remote(x_part(s, place), x_part(s, place), x_send.at[s, place], x_recv.at[s, place], sibling)

    def x_pass_on(s):
        part = x_part(s, far_source)
        return remote(part, part, x_send.at[s, z], x_recv.at[s, far_source], on_line(far_target))

    def pass_on_pixels(s):
        @pl.when(inner)
        def _():
            x_arrival(s, far_source).wait_recv()
            x_pass_on(s).start()

    def send_pixels(s):
        if s >= 2:
            each_reach(lambda place: x_copy(s - 2, place).wait_send())
        if s < blocks:
            each_reach(lambda place: x_copy(s, place).start())

    send_pixels(0)
    for copy in conv:
        copy.start()
    send_pixels(1)
    pass_on_pixels(0)
    send_pixels(2)

    forwards = []
    for d in range(1, tm_n):
        part = shard_part(lax.rem(tm - d + tm_n, tm_n), core)
        remote(part, part, conv_send.at[d - 1], conv_recv.at[d - 1], sibling).wait_recv()
        copy = remote(part, part, conv_fwd_send.at[d - 1], conv_fwd_recv.at[d - 1], sibling)
        copy.start()
        forwards.append(copy)
    own_shard.wait()
    for d in range(1, tm_n):
        part = shard_part(lax.rem(tm - d + tm_n, tm_n), 1 - core)
        remote(part, part, conv_fwd_send.at[d - 1], conv_fwd_recv.at[d - 1], sibling).wait_recv()
    for copy in own_blocks:
        copy.wait()
    pass_on_pixels(1)
    for s in range(3, blocks):
        send_pixels(s)
    kernel[...] = turned[...].T
    weights.wait()

    mine = pl.ds(pl.multiple_of(core * line_rows, line_rows), line_rows)
    other = pl.ds(pl.multiple_of((1 - core) * line_rows, line_rows), line_rows)
    hid_at = pl.multiple_of(tp * hid_local, 128)

    def h_part(s, owner):
        return hidden.at[s, :, pl.ds(pl.multiple_of(owner * hid_local, 128), hid_local)]

    def h_copy(s, place):
        return remote(h_part(s, tp), h_part(s, tp), h_send.at[s, place], h_recv.at[s, z], on_line(place))

    def h_arrival(s, place):
        part = h_part(s, place * 2 + core)
        return remote(part, part, h_send.at[s, place], h_recv.at[s, place], sibling)

    def h_pass_on(s):
        part = h_part(s, far_source * 2 + core)
        return remote(part, part, h_send.at[s, z], h_recv.at[s, far_source], on_line(far_target))

    def h_across(s, place, which):
        part = h_part(s, place * 2 + which)
        return remote(part, part, h_fwd_send.at[s, place], h_fwd_recv.at[s, place], sibling)

    def pass_on_hidden(s):
        @pl.when(inner)
        def _():
            h_arrival(s, far_source).wait_recv()
            h_pass_on(s).start()

    gain, shift = gain_ref[...].reshape(1, -1), shift_ref[...].reshape(1, -1)
    bias_in, bias_out = bias_in_ref[...].reshape(1, -1), bias_out_ref[...].reshape(1, -1)

    def embed_block(s):
        def arrived(place):
            pl.when(jnp.logical_not(inner & (far_source == place)))(lambda: x_arrival(s, place).wait_recv())

        each_source(arrived)
        tail = xs[s, :, 4 * main :].astype(jnp.float32)
        for g in range(4):
            rows = slice(g * line_rows, (g + 1) * line_rows)
            lhs[rows, :main] = xs[s, :, g * main : (g + 1) * main]
            end = pltpu.roll(tail, 128 - g * rem, 1) if g else tail
            lhs[rows, main:] = end[:, :rem].astype(jnp.bfloat16)
        for n in range(0, channels, 256):
            part = jnp.dot(lhs[...], kernel[:, n : n + 256], preferred_element_type=jnp.float32)
            embed[n // 128] = part[:, :128]
            embed[n // 128 + 1] = part[:, 128:]
        part_rows = line_rows // 2
        for i in range(2):
            for j in range(2):
                for h in range(2):
                    every = pl.ds((2 * i + h) * line_rows + j, part_rows, stride=2)
                    value = jnp.concatenate([embed[k, every, :] for k in range(channels // 128)], axis=1)
                    mean = jnp.sum(value, axis=1, keepdims=True) * (1.0 / channels)
                    centred = value - mean
                    variance = jnp.sum(centred * centred, axis=1, keepdims=True) * (1.0 / channels)
                    normed = centred * lax.rsqrt(variance + EPS) * gain + shift
                    at = pl.ds(pl.multiple_of(core * line_rows + h * part_rows, part_rows), part_rows)
                    q = 2 * i + j
                    merged[s, at, q * channels : (q + 1) * channels] = normed.astype(jnp.bfloat16)
        to_sibling = remote(merged.at[s, mine], merged.at[s, mine], m_send.at[s], m_recv.at[s], sibling)
        to_sibling.start()

    def hidden_block(s):
        remote(merged.at[s, other], merged.at[s, other], m_send.at[s], m_recv.at[s], sibling).wait_recv()
        pre = jnp.dot(merged[s], win[...], preferred_element_type=jnp.float32) + bias_in
        act = 0.5 * pre * (1.0 + lax.erf(pre * (0.5**0.5)))
        hidden[s, :, pl.ds(hid_at, hid_local)] = act.astype(jnp.bfloat16)
        each_reach(lambda place: h_copy(s, place).start())
        remote(h_part(s, tp), h_part(s, tp), h_own_send.at[s], h_own_recv.at[s], sibling).start()

    def first_half(s, carry):
        pl.when(s < blocks)(lambda: embed_block(s))
        pl.when(s + 2 < blocks)(lambda: pass_on_pixels(s + 2))
        pl.when(s > 0)(lambda: hidden_block(s - 1))
        pl.when(s > 2)(lambda: pass_on_hidden(s - 3))
        return carry

    lax.fori_loop(0, blocks + 1, first_half, 0)
    weights_out.wait()

    def hand_over(s):
        pl.when(s >= blocks - 2)(lambda: pass_on_hidden(s))
        pl.when(inner)(lambda: h_across(s, far_source, core).start())

        def arrived(place):
            @pl.when(jnp.logical_not(inner & (far_source == place)))
            def _():
                h_arrival(s, place).wait_recv()
                h_across(s, place, core).start()

        each_source(arrived)

    def second_half(s):
        part = h_part(s, z * 2 + 1 - core)
        remote(part, part, h_own_send.at[s], h_own_recv.at[s], sibling).wait_recv()
        each_source(lambda place: h_across(s, place, 1 - core).wait_recv())
        pair, band = s // bands, lax.rem(s, bands)
        for n in range(0, out_ref.shape[1], 256):
            total = jnp.dot(hidden[s], wout[:, n : n + 256], preferred_element_type=jnp.float32)
            result = total + bias_out[:, n : n + 256]
            for c in range(2):
                for l in range(line_n):
                    at = ((pair * tp_n + l * 2 + c) * bands + band) * cols
                    low = c * line_rows + l * (cols // 2)
                    high = low + line_rows // 2
                    tokens = [result[low : low + cols // 2], result[high : high + cols // 2]]
                    tokens = jnp.concatenate(tokens, axis=0).astype(jnp.bfloat16)
                    out_ref[pl.ds(pl.multiple_of(at, cols), cols), n : n + 256] = tokens

    hand_over(0)

    def finish(s, carry):
        hand_over(s)
        second_half(s - 1)
        return carry

    lax.fori_loop(1, blocks, finish, 0)
    second_half(blocks - 1)

    for copy in conv + forwards:
        copy.wait_send()

    for s in range(max(blocks, 3), blocks + 2):
        send_pixels(s)

    def drain(s, carry):
        remote(merged.at[s, mine], merged.at[s, mine], m_send.at[s], m_recv.at[s], sibling).wait_send()
        remote(h_part(s, tp), h_part(s, tp), h_own_send.at[s], h_own_recv.at[s], sibling).wait_send()
        each_reach(lambda place: h_copy(s, place).wait_send())
        each_source(lambda place: h_across(s, place, core).wait_send())

        @pl.when(inner)
        def _():
            x_pass_on(s).wait_send()
            h_pass_on(s).wait_send()

        return carry

    lax.fori_loop(0, blocks, drain, 0)


def per_device_fused(pixels, conv_weight, norm_gain, norm_bias, proj_in, bias_in, proj_out, bias_out):
    tm_n, tp_n = lax.axis_size("tm"), lax.axis_size("tp")
    pairs, rows, grid_cols, patch = pixels.shape
    channels = conv_weight.shape[1] * tm_n
    bands, cols = rows // 2, grid_cols // 2
    main = patch // 128 * 128
    rem = patch - main
    blocks = pairs * bands
    line_n = tp_n // 2
    group = tp_n * cols
    bf16 = jnp.bfloat16
    dma = pltpu.SemaphoreType.DMA
    vmem = pl.BlockSpec(memory_space=pltpu.VMEM)
    anywhere = pl.BlockSpec(memory_space=pl.ANY)
    conv_sems = [dma((tm_n - 1,))] * 4
    packed = 4 * main + 128
    line_sems = dma((blocks, line_n))
    out = pl.pallas_call(
        functools.partial(fused_kernel, (tm_n, tp_n, pairs, bands, cols, main, rem, channels)),
        out_shape=jax.ShapeDtypeStruct((blocks * group, proj_out.shape[1]), bf16),
        in_specs=[vmem] * 6 + [anywhere] * 2,
        out_specs=vmem,
        scratch_shapes=[
            pltpu.VMEM((blocks, cols, packed), bf16),
            pltpu.VMEM((blocks, line_n * cols, packed), bf16),
            pltpu.VMEM((channels, patch), bf16),
            pltpu.VMEM((patch, channels), bf16),
            pltpu.VMEM((4 * line_n * cols, patch), bf16),
            pltpu.VMEM((channels // 128, 4 * line_n * cols, 128), jnp.float32),
            pltpu.VMEM((blocks, group, 4 * channels), bf16),
            pltpu.VMEM((blocks, group, proj_out.shape[0]), bf16),
            pltpu.VMEM(proj_in.shape, bf16),
            pltpu.VMEM(proj_out.shape, bf16),
            dma((1 + blocks,)),
            dma((2,)),
        ]
        + conv_sems
        + [line_sems] * 2
        + [dma((blocks,))] * 2
        + [line_sems] * 2
        + [dma((blocks,))] * 2
        + [line_sems] * 2,
        compiler_params=pltpu.CompilerParams(
            collective_id=0, has_side_effects=True, vmem_limit_bytes=VMEM_BYTES
        ),
    )(
        pixels.reshape(blocks, 2 * grid_cols, patch), conv_weight.T,
        norm_gain, norm_bias, bias_in, bias_out, proj_in, proj_out,
    )
    return out.reshape(pairs, tp_n * bands, cols, proj_out.shape[1])


def fused_fits(pixels, conv_weight, proj_in, proj_out):
    pairs, rows, grid_cols, patch = pixels.shape
    tm_n, tp_n = lax.axis_size("tm"), lax.axis_size("tp")
    local = conv_weight.shape[1]
    held = 2 * (proj_in.size + proj_out.size) + 8 * pairs * tp_n * rows * grid_cols * local * tm_n // 2
    return (
        rows % 2 == 0
        and grid_cols % 32 == 0
        and tm_n >= 2
        and tp_n % 2 == 0
        and tp_n == 8
        and pairs * rows >= 4
        and local % 32 == 0
        and local * tm_n % 256 == 0
        and patch % 128 != 0
        and 4 * (patch % 128) <= 128
        and proj_in.shape[1] % 128 == 0
        and proj_out.shape[1] % 256 == 0
        and held < VMEM_BYTES // 3 * 2
    )


def per_device(pixels, conv_weight, norm_gain, norm_bias, proj_in, bias_in, proj_out, bias_out):
    if fused_fits(pixels, conv_weight, proj_in, proj_out):
        body = per_device_fused
    elif pixels.shape[1] % 2 == 0:
        body = per_device_whole_blocks
    else:
        body = per_device_split_blocks
    return body(pixels, conv_weight, norm_gain, norm_bias, proj_in, bias_in, proj_out, bias_out)


def solution(mesh):
    return jax.shard_map(
        per_device,
        mesh=mesh,
        in_specs=(
            P("tm", "tp", None, None),
            P(None, "tm"),
            P(),
            P(),
            P(None, "tp"),
            P("tp"),
            P(None, "tp"),
            P("tp"),
        ),
        out_specs=P("tm", None, None, "tp"),
        check_vma=False,
    )
```

```python
import functools

import jax
import jax.numpy as jnp
from jax import lax
from jax.experimental import pallas as pl
from jax.experimental.pallas import tpu as pltpu
from jax.sharding import PartitionSpec as P


def per_device_split_blocks(pixels, conv_weight, norm_gain, norm_bias, proj_in, bias_in, proj_out, bias_out):
    kernel = lax.all_gather(conv_weight, "tm", axis=1, tiled=True)
    pairs_here, rows_here, cols_all, patch_len = pixels.shape
    channels = kernel.shape[1]
    embed = jnp.dot(pixels.reshape(-1, patch_len), kernel, preferred_element_type=jnp.float32)
    mean = jnp.mean(embed, axis=-1, keepdims=True)
    centred = embed - mean
    variance = jnp.mean(centred * centred, axis=-1, keepdims=True)
    normed = (centred * lax.rsqrt(variance + 1e-06) * norm_gain + norm_bias).astype(jnp.bfloat16)
    normed = normed.reshape(pairs_here, rows_here, cols_all, channels)
    items = normed.reshape(pairs_here, rows_here, cols_all // 2, 2, channels)
    items = items.transpose(0, 2, 1, 3, 4).reshape(
        pairs_here * (cols_all // 2), rows_here, 2, channels
    )
    moved = lax.all_to_all(items, "tp", split_axis=0, concat_axis=1, tiled=True)
    owned = moved.shape[0]
    rows_full = moved.shape[1]
    merged = moved.reshape(owned, rows_full // 2, 2, 2, channels).reshape(
        owned * (rows_full // 2), 4 * channels
    )
    pre = (
        jnp.dot(
            lax.all_gather(merged, "tp", axis=0, tiled=True),
            proj_in,
            preferred_element_type=jnp.float32,
        )
        + bias_in
    )
    hidden = jax.nn.gelu(pre, approximate=False).astype(jnp.bfloat16)
    out_cols = proj_out.shape[1]
    summed = jnp.dot(
        lax.all_gather(hidden, "tp", axis=1, tiled=True),
        proj_out,
        preferred_element_type=jnp.float32,
    )
    result = (summed + bias_out).astype(jnp.bfloat16)
    result = result.reshape(pairs_here, cols_all // 2, rows_full // 2, out_cols).transpose(
        0, 2, 1, 3
    )
    return result


def per_device_whole_blocks(pixels, conv_weight, norm_gain, norm_bias, proj_in, bias_in, proj_out, bias_out):
    kernel = lax.all_gather(conv_weight, "tm", axis=1, tiled=True)
    pairs_here, rows_here, cols_all, patch_len = pixels.shape
    channels = kernel.shape[1]
    embed = jnp.dot(pixels.reshape(-1, patch_len), kernel, preferred_element_type=jnp.float32)
    mean = jnp.mean(embed, axis=-1, keepdims=True)
    centred = embed - mean
    variance = jnp.mean(centred * centred, axis=-1, keepdims=True)
    normed = (centred * lax.rsqrt(variance + 1e-06) * norm_gain + norm_bias).astype(jnp.bfloat16)
    normed = normed.reshape(pairs_here, rows_here, cols_all, channels)
    merged = normed.reshape(pairs_here, rows_here // 2, 2, cols_all // 2, 2, channels)
    merged = merged.transpose(0, 1, 3, 2, 4, 5).reshape(-1, 4 * channels)
    pre = (
        jnp.dot(
            lax.all_gather(merged, "tp", axis=0, tiled=True),
            proj_in,
            preferred_element_type=jnp.float32,
        )
        + bias_in
    )
    hidden = jax.nn.gelu(pre, approximate=False).astype(jnp.bfloat16)
    out_cols = proj_out.shape[1]
    summed = jnp.dot(
        lax.all_gather(hidden, "tp", axis=1, tiled=True),
        proj_out,
        preferred_element_type=jnp.float32,
    )
    result = (summed + bias_out).astype(jnp.bfloat16)
    tp = lax.axis_size("tp")
    result = result.reshape(tp, pairs_here, rows_here // 2, cols_all // 2, out_cols)
    result = result.transpose(1, 0, 2, 3, 4).reshape(
        pairs_here, tp * (rows_here // 2), cols_all // 2, out_cols
    )
    return result


MESH = pl.DeviceIdType.MESH
EPS = 1e-06
VMEM_BYTES = 60 * 1024 * 1024


def fused_kernel(
    dims,
    raw_ref, shard_ref, gain_ref, shift_ref, bias_in_ref, bias_out_ref, proj_in_ref, proj_out_ref,
    out_ref,
    x_ref, xs, turned, kernel, lhs, embed, merged, hidden, win, wout, total,
    own_sems, weight_sems,
    conv_send, conv_recv, conv_fwd_send, conv_fwd_recv,
    x_send, x_recv, m_send, m_recv,
    h_send, h_recv, h_own_send, h_own_recv, h_fwd_send, h_fwd_recv,
):
    tm_n, tp_n, pairs, bands, cols, main, rem, channels = dims
    line_n = tp_n // 2
    blocks = pairs * bands
    line_rows = line_n * cols
    hid_local = proj_in_ref.shape[1]
    share = shard_ref.shape[0]
    half = share // 2
    tm = lax.axis_index("tm")
    tp = lax.axis_index("tp")
    core = lax.rem(tp, 2)
    z = tp // 2
    sibling = (tm, z * 2 + 1 - core)

    def on_line(place):
        return (tm, place * 2 + core)

    last = line_n - 1
    inner = (z > 0) & (z < last)
    far_source = (2 - z) * last
    far_target = (z - 1) * last
    middle_source = last - z

    def each_reach(act):
        for e in (2, -2, 1, -1):
            place = z + e
            pl.when((place >= 0) & (place <= last))(functools.partial(act, place))

    def each_pixel_reach(act):
        for e in (2, -2, 1, -1):
            place = z + e
            inside = (place >= 0) & (place <= last)
            pl.when(inside if abs(e) == 1 else inside & jnp.logical_not(inner))(functools.partial(act, place))

    def each_source(act):
        for place in range(line_n):
            pl.when(z != place)(functools.partial(act, place))

    def along_tm(d):
        return (lax.rem(tm + d, tm_n), tp)

    def remote(src, dst, send, recv, device):
        return pltpu.make_async_remote_copy(
            src_ref=src, dst_ref=dst, send_sem=send, recv_sem=recv, device_id=device, device_id_type=MESH
        )

    barrier = pltpu.get_barrier_semaphore()
    peers = [sibling]
    peers += [on_line(lax.rem(z + d, line_n)) for d in range(1, line_n)]
    peers += [along_tm(d) for d in range(1, tm_n)]
    for peer in peers:
        pl.semaphore_signal(barrier, inc=1, device_id=peer, device_id_type=MESH)

    weights = pltpu.make_async_copy(proj_in_ref, win, weight_sems.at[0])
    weights_out = pltpu.make_async_copy(proj_out_ref, wout, weight_sems.at[1])
    own_shard = pltpu.make_async_copy(
        shard_ref, turned.at[pl.ds(pl.multiple_of(tm * share, 16), share)], own_sems.at[0]
    )
    for copy in (own_shard, weights, weights_out):
        copy.start()

    lane = lax.broadcasted_iota(jnp.int32, (cols, 128), 1)
    for s in range(blocks):
        tail = jnp.zeros((cols, 128), jnp.float32)
        for g in range(4):
            rows = slice(g * cols, (g + 1) * cols)
            x_ref[s, :, g * main : (g + 1) * main] = raw_ref[s, rows, :main]
            end = raw_ref[s, rows, main:].astype(jnp.float32)
            end = jnp.concatenate([end, jnp.zeros((cols, 128 - rem), jnp.float32)], axis=1)
            tail += pltpu.roll(end, g * rem, 1) if g else end
        x_ref[s, :, 4 * main :] = tail.astype(jnp.bfloat16)
    own_blocks = [
        pltpu.make_async_copy(
            x_ref.at[s], xs.at[s, pl.ds(pl.multiple_of(z * cols, cols), cols)], own_sems.at[1 + s]
        )
        for s in range(blocks)
    ]
    for copy in own_blocks:
        copy.start()

    pl.semaphore_wait(barrier, len(peers))

    def shard_part(owner, which):
        return turned.at[pl.ds(pl.multiple_of(owner * share + which * half, 16), half)]

    conv = [
        remote(
            shard_ref.at[pl.ds(pl.multiple_of(core * half, 16), half)],
            shard_part(tm, core), conv_send.at[d - 1], conv_recv.at[d - 1], along_tm(d),
        )
        for d in range(1, tm_n)
    ]

    def x_part(s, place):
        return xs.at[s, pl.ds(pl.multiple_of(place * cols, cols), cols)]

    def x_copy(s, place):
        return remote(
            x_ref.at[s], x_part(s, z), x_send.at[s, place], x_recv.at[s, z], on_line(place)
        )

    def x_arrival(s, place):
        return remote(x_part(s, place), x_part(s, place), x_send.at[s, place], x_recv.at[s, place], sibling)

    def x_pass_on(s, source, sem):
        part = x_part(s, source)
        return remote(part, part, x_send.at[s, sem], x_recv.at[s, source], on_line(far_target))

    def pass_on_pixels(s):
        @pl.when(inner)
        def _():
            x_arrival(s, middle_source).wait_recv()
            x_pass_on(s, middle_source, far_source).start()
            x_arrival(s, far_source).wait_recv()
            x_pass_on(s, far_source, z).start()

    for s in range(blocks):
        each_pixel_reach(lambda place, s=s: x_copy(s, place).start())
        for copy in conv[s : s + 1]:
            copy.start()
    for copy in conv[blocks:]:
        copy.start()
    pass_on_pixels(0)
    pass_on_pixels(1)

    forwards = []
    for d in range(1, tm_n):
        part = shard_part(lax.rem(tm - d + tm_n, tm_n), core)
        remote(part, part, conv_send.at[d - 1], conv_recv.at[d - 1], sibling).wait_recv()
        copy = remote(part, part, conv_fwd_send.at[d - 1], conv_fwd_recv.at[d - 1], sibling)
        copy.start()
        forwards.append(copy)
    own_shard.wait()
    for d in range(1, tm_n):
        part = shard_part(lax.rem(tm - d + tm_n, tm_n), 1 - core)
        remote(part, part, conv_fwd_send.at[d - 1], conv_fwd_recv.at[d - 1], sibling).wait_recv()
    for copy in own_blocks:
        copy.wait()
    pl.when(blocks > 2)(lambda: pass_on_pixels(2))
    kernel[...] = turned[...].T
    weights.wait()

    mine = pl.ds(pl.multiple_of(core * line_rows, line_rows), line_rows)
    other = pl.ds(pl.multiple_of((1 - core) * line_rows, line_rows), line_rows)
    hid_at = pl.multiple_of(tp * hid_local, 128)

    def h_part(s, owner):
        return hidden.at[s, :, pl.ds(pl.multiple_of(owner * hid_local, 128), hid_local)]

    def h_copy(s, place):
        return remote(h_part(s, tp), h_part(s, tp), h_send.at[s, place], h_recv.at[s, z], on_line(place))

    def h_arrival(s, place):
        part = h_part(s, place * 2 + core)
        return remote(part, part, h_send.at[s, place], h_recv.at[s, place], sibling)

    def h_pass_on(s):
        part = h_part(s, far_source * 2 + core)
        return remote(part, part, h_send.at[s, z], h_recv.at[s, far_source], on_line(far_target))

    def h_across(s, place, which):
        part = h_part(s, place * 2 + which)
        return remote(part, part, h_fwd_send.at[s, place], h_fwd_recv.at[s, place], sibling)

    def pass_on_hidden(s):
        @pl.when(inner)
        def _():
            h_arrival(s, far_source).wait_recv()
            h_pass_on(s).start()

    gain, shift = gain_ref[...].reshape(1, -1), shift_ref[...].reshape(1, -1)
    bias_in, bias_out = bias_in_ref[...].reshape(1, -1), bias_out_ref[...].reshape(1, -1)

    def embed_block(s):
        def arrived(place):
            passed = inner & ((far_source == place) | (middle_source == place))
            pl.when(jnp.logical_not(passed))(lambda: x_arrival(s, place).wait_recv())

        each_source(arrived)
        tail = xs[s, :, 4 * main :].astype(jnp.float32)
        for g in range(4):
            rows = slice(g * line_rows, (g + 1) * line_rows)
            lhs[rows, :main] = xs[s, :, g * main : (g + 1) * main]
            end = pltpu.roll(tail, 128 - g * rem, 1) if g else tail
            lhs[rows, main:] = end[:, :rem].astype(jnp.bfloat16)
        for n in range(0, channels, 256):
            part = jnp.dot(lhs[...], kernel[:, n : n + 256], preferred_element_type=jnp.float32)
            embed[n // 128] = part[:, :128]
            embed[n // 128 + 1] = part[:, 128:]
        part_rows = line_rows // 2
        for i in range(2):
            for j in range(2):
                for h in range(2):
                    every = pl.ds((2 * i + h) * line_rows + j, part_rows, stride=2)
                    value = jnp.concatenate([embed[k, every, :] for k in range(channels // 128)], axis=1)
                    mean = jnp.sum(value, axis=1, keepdims=True) * (1.0 / channels)
                    centred = value - mean
                    variance = jnp.sum(centred * centred, axis=1, keepdims=True) * (1.0 / channels)
                    normed = centred * lax.rsqrt(variance + EPS) * gain + shift
                    at = pl.ds(pl.multiple_of(core * line_rows + h * part_rows, part_rows), part_rows)
                    q = 2 * i + j
                    merged[s, at, q * channels : (q + 1) * channels] = normed.astype(jnp.bfloat16)
        to_sibling = remote(merged.at[s, mine], merged.at[s, mine], m_send.at[s], m_recv.at[s], sibling)
        to_sibling.start()

    def hidden_block(s):
        remote(merged.at[s, other], merged.at[s, other], m_send.at[s], m_recv.at[s], sibling).wait_recv()
        pre = jnp.dot(merged[s], win[...], preferred_element_type=jnp.float32) + bias_in
        act = 0.5 * pre * (1.0 + lax.erf(pre * (0.5**0.5)))
        hidden[s, :, pl.ds(hid_at, hid_local)] = act.astype(jnp.bfloat16)
        each_reach(lambda place: h_copy(s, place).start())
        remote(h_part(s, tp), h_part(s, tp), h_own_send.at[s], h_own_recv.at[s], sibling).start()

    def first_half(s, carry):
        pl.when(s < blocks)(lambda: embed_block(s))
        pl.when(s + 3 < blocks)(lambda: pass_on_pixels(s + 3))
        pl.when(s > 0)(lambda: hidden_block(s - 1))
        pl.when(s > 2)(lambda: pass_on_hidden(s - 3))
        return carry

    lax.fori_loop(0, blocks + 1, first_half, 0)
    weights_out.wait()

    def hand_over(s):
        pl.when(s >= blocks - 2)(lambda: pass_on_hidden(s))
        pl.when(inner)(lambda: h_across(s, far_source, core).start())

        def arrived(place):
            @pl.when(jnp.logical_not(inner & (far_source == place)))
            def _():
                h_arrival(s, place).wait_recv()
                h_across(s, place, core).start()

        each_source(arrived)

    def second_half(s):
        part = h_part(s, z * 2 + 1 - core)
        remote(part, part, h_own_send.at[s], h_own_recv.at[s], sibling).wait_recv()
        each_source(lambda place: h_across(s, place, 1 - core).wait_recv())
        for n in range(0, out_ref.shape[1], 256):
            product = jnp.dot(hidden[s], wout[:, n : n + 256], preferred_element_type=jnp.float32)
            put_tokens(s, n, product + bias_out[:, n : n + 256])

    def put_tokens(s, n, result):
        pair, band = s // bands, lax.rem(s, bands)
        for c in range(2):
            for l in range(line_n):
                at = ((pair * tp_n + l * 2 + c) * bands + band) * cols
                low = c * line_rows + l * (cols // 2)
                high = low + line_rows // 2
                tokens = [result[low : low + cols // 2], result[high : high + cols // 2]]
                tokens = jnp.concatenate(tokens, axis=0).astype(jnp.bfloat16)
                out_ref[pl.ds(pl.multiple_of(at, cols), cols), n : n + 256] = tokens

    def last_block(s):
        def take(place):
            pl.when(jnp.logical_not(inner & (far_source == place)))(lambda: h_arrival(s, place).wait_recv())
            h_across(s, place, core).start()

        def add(place):
            at = pl.multiple_of(place * 2 * hid_local, 128)
            for n in range(0, out_ref.shape[1], 256):
                part = jnp.dot(
                    hidden[s, :, pl.ds(at, 2 * hid_local)],
                    wout[pl.ds(at, 2 * hid_local), n : n + 256],
                    preferred_element_type=jnp.float32,
                )
                total[:, n : n + 256] += part

        upper = z // 2
        order = (1 - z + 4 * upper, 2 - upper, 3 - 3 * upper)
        total[...] = jnp.broadcast_to(bias_out, total.shape)
        pass_on_hidden(s)
        part = h_part(s, z * 2 + 1 - core)
        remote(part, part, h_own_send.at[s], h_own_recv.at[s], sibling).wait_recv()
        ready = z
        for place in order:
            take(place)
            add(ready)
            h_across(s, place, 1 - core).wait_recv()
            ready = place
        add(ready)
        for n in range(0, out_ref.shape[1], 256):
            put_tokens(s, n, total[:, n : n + 256])

    hand_over(0)

    def finish(s, carry):
        hand_over(s)
        second_half(s - 1)
        return carry

    lax.fori_loop(1, blocks - 1, finish, 0)
    second_half(blocks - 2)
    last_block(blocks - 1)

    for copy in conv + forwards:
        copy.wait_send()

    def drain(s, carry):
        remote(merged.at[s, mine], merged.at[s, mine], m_send.at[s], m_recv.at[s], sibling).wait_send()
        remote(h_part(s, tp), h_part(s, tp), h_own_send.at[s], h_own_recv.at[s], sibling).wait_send()
        each_pixel_reach(lambda place: x_copy(s, place).wait_send())
        each_reach(lambda place: h_copy(s, place).wait_send())
        each_source(lambda place: h_across(s, place, core).wait_send())

        @pl.when(inner)
        def _():
            x_pass_on(s, middle_source, far_source).wait_send()
            x_pass_on(s, far_source, z).wait_send()
            h_pass_on(s).wait_send()

        return carry

    lax.fori_loop(0, blocks, drain, 0)


def per_device_fused(pixels, conv_weight, norm_gain, norm_bias, proj_in, bias_in, proj_out, bias_out):
    tm_n, tp_n = lax.axis_size("tm"), lax.axis_size("tp")
    pairs, rows, grid_cols, patch = pixels.shape
    channels = conv_weight.shape[1] * tm_n
    bands, cols = rows // 2, grid_cols // 2
    main = patch // 128 * 128
    rem = patch - main
    blocks = pairs * bands
    line_n = tp_n // 2
    group = tp_n * cols
    bf16 = jnp.bfloat16
    dma = pltpu.SemaphoreType.DMA
    vmem = pl.BlockSpec(memory_space=pltpu.VMEM)
    anywhere = pl.BlockSpec(memory_space=pl.ANY)
    conv_sems = [dma((tm_n - 1,))] * 4
    packed = 4 * main + 128
    line_sems = dma((blocks, line_n))
    out = pl.pallas_call(
        functools.partial(fused_kernel, (tm_n, tp_n, pairs, bands, cols, main, rem, channels)),
        out_shape=jax.ShapeDtypeStruct((blocks * group, proj_out.shape[1]), bf16),
        in_specs=[vmem] * 6 + [anywhere] * 2,
        out_specs=vmem,
        scratch_shapes=[
            pltpu.VMEM((blocks, cols, packed), bf16),
            pltpu.VMEM((blocks, line_n * cols, packed), bf16),
            pltpu.VMEM((channels, patch), bf16),
            pltpu.VMEM((patch, channels), bf16),
            pltpu.VMEM((4 * line_n * cols, patch), bf16),
            pltpu.VMEM((channels // 128, 4 * line_n * cols, 128), jnp.float32),
            pltpu.VMEM((blocks, group, 4 * channels), bf16),
            pltpu.VMEM((blocks, group, proj_out.shape[0]), bf16),
            pltpu.VMEM(proj_in.shape, bf16),
            pltpu.VMEM(proj_out.shape, bf16),
            pltpu.VMEM((group, proj_out.shape[1]), jnp.float32),
            dma((1 + blocks,)),
            dma((2,)),
        ]
        + conv_sems
        + [line_sems] * 2
        + [dma((blocks,))] * 2
        + [line_sems] * 2
        + [dma((blocks,))] * 2
        + [line_sems] * 2,
        compiler_params=pltpu.CompilerParams(
            collective_id=0, has_side_effects=True, vmem_limit_bytes=VMEM_BYTES
        ),
    )(
        pixels.reshape(blocks, 2 * grid_cols, patch), conv_weight.T,
        norm_gain, norm_bias, bias_in, bias_out, proj_in, proj_out,
    )
    return out.reshape(pairs, tp_n * bands, cols, proj_out.shape[1])


def fused_fits(pixels, conv_weight, proj_in, proj_out):
    pairs, rows, grid_cols, patch = pixels.shape
    tm_n, tp_n = lax.axis_size("tm"), lax.axis_size("tp")
    local = conv_weight.shape[1]
    held = 2 * (proj_in.size + proj_out.size) + 8 * pairs * tp_n * rows * grid_cols * local * tm_n // 2
    return (
        rows % 2 == 0
        and grid_cols % 32 == 0
        and tm_n >= 2
        and tp_n % 2 == 0
        and tp_n == 8
        and pairs * rows >= 6
        and local % 32 == 0
        and local * tm_n % 256 == 0
        and patch % 128 != 0
        and 4 * (patch % 128) <= 128
        and proj_in.shape[1] % 128 == 0
        and proj_out.shape[1] % 256 == 0
        and held < VMEM_BYTES // 3 * 2
    )


def per_device(pixels, conv_weight, norm_gain, norm_bias, proj_in, bias_in, proj_out, bias_out):
    if fused_fits(pixels, conv_weight, proj_in, proj_out):
        body = per_device_fused
    elif pixels.shape[1] % 2 == 0:
        body = per_device_whole_blocks
    else:
        body = per_device_split_blocks
    return body(pixels, conv_weight, norm_gain, norm_bias, proj_in, bias_in, proj_out, bias_out)


def solution(mesh):
    return jax.shard_map(
        per_device,
        mesh=mesh,
        in_specs=(
            P("tm", "tp", None, None),
            P(None, "tm"),
            P(),
            P(),
            P(None, "tp"),
            P("tp"),
            P(None, "tp"),
            P("tp"),
        ),
        out_specs=P("tm", None, None, "tp"),
        check_vma=False,
    )
```
